256 devices in a mesh: state: 4 (over y), frame: 64 (over x, z, core).
Axes of the slice: x: 4, y: 4, z: 8, core: 2. Of those that a mesh axis runs over, the one named last changes fastest.
Arguments:
- energies: float32 [512, 524288], P('state', 'frame'), may hold values from -195 to 215, as said below
- sample_counts: int32 [512], P('state'), may hold values from 1 to 4096, 524288 in all
- state_leg: int32 [512], P('state'), may hold values from 0 to 7, never falling along the last dimension, each value on 1 to 128 neighbouring positions
- bin_index: int32 [524288, 6, 8], P('frame'), may hold values from 0 to 255
Outputs:
- rdf: float32 [1536, 512], P('frame', 'state')
- leg_free: float32 [512], P('state')
The draws below stay inside these ranges and needn't reach their ends.
Inputs may be any that keep to these rules, and one draw needn't show every extreme that they name: The energies of the shown and hidden draws lie in this range. `sample_counts`: the counts sum to 524288. `state_leg`: each group is a nonempty run of consecutive states, numbered in order.
All inputs are finite; a program needn't handle non-finite values. No bound on the sum of `sample_counts` on one device may be relied on, other than what follows from the above.
Results may differ from the reference program's by a relative error of at most 0.0003.
Values sent between devices are 32-bit elements; how exact they have to be, the bound alone decides.
A program may use at most 64 MiB of HBM per device.

```python
import math
import jax
import jax.numpy as jnp
import numpy as np
from jax import lax

STATES = 512
BINS = 256
TYPES = 6
PAIRS = 8
LEGS = 8
ITERS = 2
FRAMES = 524288


def draw_energies(key, part):
    key = jax.random.fold_in(key, 11)
    keys = jax.random.split(key, 5)
    jitter = jax.random.uniform(keys[0], (1, FRAMES), jnp.float32)
    frame_order = jnp.arange(FRAMES, dtype=jnp.int32).astype(jnp.float32)[None, :]
    position = (frame_order + jitter) / float(FRAMES)
    centre = jax.random.uniform(keys[1], (STATES, 1), jnp.float32)
    offset = jax.random.uniform(keys[2], (STATES, 1), jnp.float32, -3.0, 3.0)
    shift = jnp.zeros((1, FRAMES), jnp.float32)
    noise = jnp.clip(jax.random.normal(keys[4], (STATES, FRAMES), jnp.float32), -6.0, 6.0)
    spread = position - centre
    return (offset + shift + 20.0 * spread * spread + noise).astype(jnp.float32)


def place_ends(result, key, smallest, high):
    longest = result.shape.index(max(result.shape))
    spots = []
    for shift in (0, 1):
        where = [jax.random.randint(jax.random.fold_in(key, axis), (), 0, length) for axis, length in enumerate(result.shape)]
        where[longest] = (where[longest] + shift) % result.shape[longest]
        spots.append(tuple(where))
    return result.at[spots[0]].set(smallest).at[spots[1]].set(high)


def split_up(number_of, total, most, lean):
    weights = [(1 << 20) // math.isqrt(grade ** lean) + 1 for grade in range(2, number_of + 1)]
    surplus, given = total - most - (number_of - 1), [1] * (number_of - 1)
    while surplus > 0:
        candidates = [i for i in range(number_of - 1) if given[i] < most]
        mass, left = sum([weights[i] for i in candidates]), surplus
        for i in candidates:
            more = min(most - given[i], max(1, left * weights[i] // mass), surplus)
            given[i] = given[i] + more
            surplus = surplus - more
    return np.array([most] + given)


def ragged(own_key, number_of, total, limit, lean):
    if number_of == 2:
        one = jax.random.randint(own_key, (), max(1, total - limit), min(limit, total - 1) + 1)
        return jnp.stack([one, total - one])
    sizes = jnp.asarray(split_up(number_of, total, limit, lean), jnp.int32)
    couples = (number_of - 1) // 2
    giver, taker = sizes[1:1 + 2 * couples:2], sizes[2:2 + 2 * couples:2]
    room = jnp.minimum(giver - 1, limit - taker)
    moved = jax.random.randint(jax.random.fold_in(own_key, 1), (couples,), 0, 1 << 20) % (room + 1)
    sizes = sizes.at[1:1 + 2 * couples:2].set(giver - moved).at[2:2 + 2 * couples:2].set(taker + moved)
    return sizes[jax.random.permutation(jax.random.fold_in(own_key, 2), number_of)]


def setup_inputs(seed: int = 0) -> dict:
    arg_keys = jax.random.split(jax.random.key(seed), 5)
    energies = draw_energies(jax.random.fold_in(arg_keys[4], 71), 0)
    sample_counts = ragged(arg_keys[1], STATES, FRAMES, 4 * FRAMES // STATES, 2).astype(jnp.int32)
    state_leg = jnp.searchsorted(jnp.cumsum(ragged(arg_keys[2], LEGS, STATES, STATES // 4, 2)), jnp.arange(STATES), side="right").astype(jnp.int32)
    bin_index = place_ends(jax.random.randint(arg_keys[3], (FRAMES, TYPES, PAIRS), 0, BINS), jax.random.fold_in(arg_keys[3], 1), 0, BINS - 1).astype(jnp.int32)
    return {"energies": energies, "sample_counts": sample_counts, "state_leg": state_leg, "bin_index": bin_index}


def log_sum_exp(values, axis):
    largest = jnp.max(values, axis=axis, keepdims=True)
    totals = jnp.sum(jnp.exp(values - largest), axis=axis)
    return jnp.squeeze(largest, axis) + jnp.log(totals)


def reference(energies, sample_counts, state_leg, bin_index):
    log_counts = jnp.log(sample_counts.astype(jnp.float32))
    free_energy = jnp.zeros((STATES,), jnp.float32)
    for iteration in range(ITERS):
        log_denominator = log_sum_exp((log_counts + free_energy)[:, None] - energies, 0)
        free_energy = -log_sum_exp(-energies - log_denominator[None, :], 1)
    final_denominator = log_sum_exp((log_counts + free_energy)[:, None] - energies, 0)
    weights = jnp.exp(free_energy[:, None] - energies - final_denominator[None, :]).astype(jnp.bfloat16)
    block = min(4096, FRAMES)
    bin_range = jnp.arange(BINS, dtype=jnp.int32)

    def add_block(index, total):
        rows = lax.dynamic_slice_in_dim(bin_index, (index * block).astype(jnp.int32), block, 0)
        weight_block = lax.dynamic_slice_in_dim(weights, (index * block).astype(jnp.int32), block, 1)
        pair_counts = jnp.sum((rows[:, :, :, None] == bin_range[None, None, None, :]).astype(jnp.int32), axis=2)
        pair_counts = pair_counts.reshape(block, TYPES * BINS).astype(jnp.bfloat16)
        return total + jnp.dot(weight_block, pair_counts, preferred_element_type=jnp.float32)

    histogram = lax.fori_loop(0, FRAMES // block, add_block, jnp.zeros((STATES, TYPES * BINS), jnp.float32))
    rdf = histogram.T * (BINS / PAIRS)
    leg_table = (state_leg[:, None] == jnp.arange(LEGS, dtype=jnp.int32)[None, :]).astype(jnp.float32)
    leg_mean = jnp.sum(leg_table * free_energy[:, None], axis=0) / jnp.sum(leg_table, axis=0)
    leg_free = free_energy - jnp.sum(leg_table * leg_mean[None, :], axis=1)
    return rdf, leg_free
```

```python
import functools

import jax
import jax.numpy as jnp
from jax import lax
from jax.experimental import pallas as pl
from jax.experimental.pallas import tpu as pltpu
from jax.sharding import PartitionSpec as P

BINS = 256
TYPES = 6
PAIRS = 8
LEGS = 8
ITERS = 2
YS = 4
XS = 4
ZS = 8
FS = XS * ZS * 2
LANES = 128
ROWS = 128
COLS = 8192
BLOCKS = COLS // LANES
OWN = TYPES * BINS // FS
PARTS = 4
WIDE = 256
MESH = pl.DeviceIdType.MESH


def eye():
    shape = (ROWS, LANES)
    return lax.broadcasted_iota(jnp.int32, shape, 0) == lax.broadcasted_iota(jnp.int32, shape, 1)


def to_col(row):
    return jnp.sum(jnp.where(eye(), jnp.broadcast_to(row, (ROWS, LANES)), 0.0), axis=1, keepdims=True)


def to_row(col):
    return jnp.sum(jnp.where(eye(), jnp.broadcast_to(col, (ROWS, LANES)), 0.0), axis=0, keepdims=True)


def place(row):
    group, rest = divmod(row, 2 * OWN)
    x, z = divmod(group, ZS)
    return z * (XS * 2 * OWN) + x * 2 * OWN + rest


def count_block(bins, counts, block):
    cols = pl.ds(pl.multiple_of(block * WIDE, WIDE), WIDE)
    iota = lax.broadcasted_iota(jnp.int32, (16, WIDE), 0)
    for t in range(TYPES):
        rows = bins[t, :, cols]
        low = rows & 15
        one = jnp.left_shift(1, (rows >> 4) * 2)
        even = odd = None
        for group in ((0, 1, 2), (3, 4, 5), (6, 7)):
            word = None
            for p in group:
                hot = jnp.where(low[p : p + 1] == iota, one[p : p + 1], 0)
                word = hot if word is None else word + hot
            a = word & 0x33333333
            b = lax.shift_right_logical(word, 2) & 0x33333333
            even = a if even is None else even + a
            odd = b if odd is None else odd + b
        for half, nibbles in ((0, even), (16, odd)):
            for q in range(0, 8, 2):
                v = lax.shift_right_logical(nibbles, 4 * q) if q else nibbles
                if q < 6:
                    v = v & 255
                v = v.astype(jnp.float32).astype(jnp.bfloat16)
                upper = (v + jnp.bfloat16(2048)) - jnp.bfloat16(2048)
                base = t * BINS + 32 * q + half
                counts[pl.ds(place(base), 16), cols] = v - upper
                counts[pl.ds(place(base + 32), 16), cols] = upper * jnp.bfloat16(0.0625)


def kernel(
    e_hbm, n_ref, leg_ref, bins_hbm, out_ref, leg_out,
    energies, bins, counts, weights, acol, mbuf, sbuf, dbuf,
    ybuf, fbuf, legbuf, part, crecv, xsend, xrecv, zsend, zrecv,
    e_sem, bins_sem, ysend_sem, yrecv_sem, fsend_sem, frecv_sem, legsend_sem, legrecv_sem,
    csend_sem, crecv_sem, xsend_sem, xrecv_sem, zsend_sem, zrecv_sem,
):
    y = lax.axis_index("state")
    f = lax.axis_index("frame")
    core = lax.rem(f, 2)
    z = lax.rem(lax.div(f, 2), ZS)
    x = lax.div(f, 2 * ZS)
    width = COLS // PARTS

    loads = [
        pltpu.make_async_copy(
            e_hbm.at[:, pl.ds(i * width, width)], energies.at[:, pl.ds(i * width, width)], e_sem.at[i]
        )
        for i in range(PARTS)
    ]
    for load in loads:
        load.start()
    bins_load = pltpu.make_async_copy(bins_hbm, bins, bins_sem)
    bins_load.start()

    barrier = pltpu.get_barrier_semaphore()

    def greet(d, _):
        pl.semaphore_signal(barrier, inc=1, device_id=(y, lax.rem(f + d, FS)), device_id_type=MESH)
        return 0

    for d in range(1, YS):
        pl.semaphore_signal(barrier, inc=1, device_id=(lax.rem(y + d, YS), f), device_id_type=MESH)
    lax.fori_loop(1, FS, greet, 0)

    def count(first, last):
        def body(b, _):
            count_block(bins, counts, b)
            return 0

        lax.fori_loop(first, last, body, 0)

    def set_terms(row):
        acol[...] = jnp.broadcast_to(to_col(row), (ROWS, LANES))

    def state_pass(first, last):
        def body(j, _):
            cols = pl.ds(pl.multiple_of(j * LANES, LANES), LANES)
            scores = acol[...] - energies[:, cols]
            largest = jnp.max(scores, axis=0, keepdims=True)
            mbuf[pl.ds(j, 1), :] = largest
            sbuf[pl.ds(j, 1), :] = jnp.sum(jnp.exp(scores - largest), axis=0, keepdims=True)
            return 0

        lax.fori_loop(first, last, body, 0, unroll=2)

    def y_copy(stage, d):
        return pltpu.make_async_remote_copy(
            src_ref=ybuf.at[stage, y], dst_ref=ybuf.at[stage, y],
            send_sem=ysend_sem.at[stage], recv_sem=yrecv_sem.at[stage],
            device_id=(lax.rem(y + d, YS), f), device_id_type=MESH,
        )

    def y_start(stage):
        ybuf[stage, y] = mbuf[...] + jnp.log(sbuf[...])

    def y_send(stage):
        for d in (2, 1, 3):
            y_copy(stage, d).start()

    def y_finish(stage):
        got = ybuf.at[stage, pl.ds(0, YS - 1)]
        pltpu.make_async_copy(got, got, yrecv_sem.at[stage]).wait()
        parts = [ybuf[stage, k] for k in range(YS)]
        largest = functools.reduce(jnp.maximum, parts)
        total = functools.reduce(jnp.add, [jnp.exp(part - largest) for part in parts])
        dbuf[...] = largest + jnp.log(total)

    def frame_pass(stage):
        def smallest(j, least):
            cols = pl.ds(pl.multiple_of(j * LANES, LANES), LANES)
            return jnp.minimum(least, energies[:, cols] + dbuf[pl.ds(j, 1), :])

        least = lax.fori_loop(
            0, BLOCKS, smallest, jnp.full((ROWS, LANES), jnp.inf, jnp.float32), unroll=2
        )
        least = jnp.min(least, axis=1, keepdims=True)
        acol[...] = jnp.broadcast_to(least, (ROWS, LANES))

        def add(j, total):
            cols = pl.ds(pl.multiple_of(j * LANES, LANES), LANES)
            return total + jnp.exp(acol[...] - (energies[:, cols] + dbuf[pl.ds(j, 1), :]))

        total = lax.fori_loop(0, BLOCKS, add, jnp.zeros((ROWS, LANES), jnp.float32), unroll=2)
        total = jnp.sum(total, axis=1, keepdims=True)
        fbuf[stage, f] = to_row(jnp.log(total) - least)

    def f_send(stage):
        def start(d, _):
            pltpu.make_async_remote_copy(
                src_ref=fbuf.at[stage, f], dst_ref=fbuf.at[stage, f],
                send_sem=fsend_sem.at[stage], recv_sem=frecv_sem.at[stage],
                device_id=(y, lax.rem(f + d, FS)), device_id_type=MESH,
            ).start()
            return 0

        lax.fori_loop(1, FS, start, 0)

    def f_finish(stage):
        got = fbuf.at[stage, pl.ds(0, FS - 1)]
        pltpu.make_async_copy(got, got, frecv_sem.at[stage]).wait()
        parts = fbuf[stage]
        largest = jnp.max(parts, axis=0)
        return -(largest + jnp.log(jnp.sum(jnp.exp(parts - largest[None]), axis=0)))

    log_counts = jnp.log(n_ref[...].astype(jnp.float32))
    set_terms(log_counts)
    for i in range(PARTS):
        loads[i].wait()
        state_pass(i * BLOCKS // PARTS, (i + 1) * BLOCKS // PARTS)
    y_start(0)
    bins_load.wait()
    blocks = COLS // WIDE
    count(0, blocks // 4)
    pl.semaphore_wait(barrier, YS - 1 + FS - 1)
    y_send(0)
    count(blocks // 4, blocks // 2)
    y_finish(0)
    frame_pass(0)
    f_send(0)
    count(blocks // 2, blocks)
    free = f_finish(0)

    set_terms(log_counts + free)
    state_pass(0, BLOCKS)
    y_start(1)
    y_send(1)
    y_finish(1)
    frame_pass(1)
    f_send(1)
    free = f_finish(1)

    set_terms(log_counts + free)
    state_pass(0, BLOCKS)
    y_start(2)
    y_send(2)
    free_col = to_col(free)
    leg_col = to_col(leg_ref[...].astype(jnp.float32))
    lane = lax.broadcasted_iota(jnp.int32, (ROWS, LANES), 1).astype(jnp.float32)
    table = (jnp.broadcast_to(leg_col, (ROWS, LANES)) == lane).astype(jnp.float32)
    legbuf[y, 0:1] = jnp.sum(table * free_col, axis=0, keepdims=True)
    legbuf[y, 1:2] = jnp.sum(table, axis=0, keepdims=True)
    for d in range(1, YS):
        pltpu.make_async_remote_copy(
            src_ref=legbuf.at[y], dst_ref=legbuf.at[y],
            send_sem=legsend_sem, recv_sem=legrecv_sem,
            device_id=(lax.rem(y + d, YS), f), device_id_type=MESH,
        ).start()
    acol[...] = jnp.broadcast_to(free_col, (ROWS, LANES))
    y_finish(2)

    def weigh(j, _):
        cols = pl.ds(pl.multiple_of(j * LANES, LANES), LANES)
        value = jnp.exp((acol[...] - energies[:, cols]) - dbuf[pl.ds(j, 1), :])
        weights[:, cols] = value.astype(jnp.bfloat16)
        return 0

    lax.fori_loop(0, BLOCKS, weigh, 0, unroll=2)

    def offset(s):
        return 4 + (1 - 2 * lax.rem(s, 2)) * lax.div(s + 1, 2)

    def core_copy(s):
        other = 1 - core
        return pltpu.make_async_remote_copy(
            src_ref=part.at[s, :, other], dst_ref=crecv.at[s],
            send_sem=csend_sem, recv_sem=crecv_sem.at[s],
            device_id=(y, f + 1 - 2 * core), device_id_type=MESH,
        )

    def x_copy(s, d):
        to = lax.rem(x + d, XS)
        return pltpu.make_async_remote_copy(
            src_ref=xsend.at[s, to], dst_ref=xrecv.at[s, d - 1],
            send_sem=xsend_sem, recv_sem=xrecv_sem.at[s],
            device_id=(y, to * (2 * ZS) + z * 2 + core), device_id_type=MESH,
        )

    def z_copy(s):
        to = lax.rem(z + offset(s), ZS)
        return pltpu.make_async_remote_copy(
            src_ref=zsend.at[s], dst_ref=zrecv.at[s],
            send_sem=zsend_sem, recv_sem=zrecv_sem,
            device_id=(y, x * (2 * ZS) + to * 2 + core), device_id_type=MESH,
        )

    def core_post(s):
        pltpu.make_async_copy(crecv.at[s], crecv.at[s], crecv_sem.at[s]).wait()
        xsend[s] = part[s, :, core] + crecv[s]
        for d in (2, 1, 3):
            x_copy(s, d).start()

    def x_post(s):
        pltpu.make_async_copy(xrecv.at[s], xrecv.at[s], xrecv_sem.at[s]).wait()
        zsend[s] = (xsend[s, x] + xrecv[s, 0]) + (xrecv[s, 1] + xrecv[s, 2])

    def x_post_send(s):
        x_post(s)
        z_copy(s).start()

    lag = 5

    def step(s, _):
        rows = pl.ds(pl.multiple_of(lax.rem(z + offset(s), ZS) * (XS * 2 * OWN), 32), XS * 2 * OWN)
        result = lax.dot_general(
            counts[rows, :], weights[...], (((1,), (1,)), ((), ())), preferred_element_type=jnp.float32
        )
        part[s] = result.reshape(XS, 2, OWN, LANES)
        core_copy(s).start()

        @pl.when(s >= 1)
        def _():
            core_post(s - 1)

        @pl.when(s >= lag)
        def _():
            x_post_send(s - lag)

        return 0

    lax.fori_loop(0, ZS, step, 0)
    core_post(ZS - 1)

    got = legbuf.at[pl.ds(0, YS - 1)]
    pltpu.make_async_copy(got, got, legrecv_sem).wait()
    legs = (legbuf[0] + legbuf[1]) + (legbuf[2] + legbuf[3])
    leg_mean = legs[0:1] / jnp.maximum(legs[1:2], 1.0)
    leg_out[...] = to_row(
        acol[:, 0:1] - jnp.sum(table * jnp.broadcast_to(leg_mean, (ROWS, LANES)), axis=1, keepdims=True)
    )

    def late(s, _):
        x_post_send(s)
        return 0

    lax.fori_loop(ZS - lag, ZS - 1, late, 0)
    x_post(ZS - 1)
    got = zrecv.at[pl.ds(0, ZS - 1)]
    pltpu.make_async_copy(got, got, zrecv_sem).wait()
    total = zsend[ZS - 1]
    for s in range(ZS - 1):
        total = total + zrecv[s]
    out_ref[...] = total * (BINS / PAIRS)

    for stage in range(ITERS + 1):
        sent = ybuf.at[stage, pl.ds(0, YS - 1)]
        pltpu.make_async_copy(sent, sent, ysend_sem.at[stage]).wait()
    for stage in range(ITERS):
        sent = fbuf.at[stage, pl.ds(0, FS - 1)]
        pltpu.make_async_copy(sent, sent, fsend_sem.at[stage]).wait()
    sent = legbuf.at[pl.ds(0, YS - 1)]
    pltpu.make_async_copy(sent, sent, legsend_sem).wait()
    pltpu.make_async_copy(crecv, crecv, csend_sem).wait()
    pltpu.make_async_copy(xrecv, xrecv, xsend_sem).wait()
    sent = zrecv.at[pl.ds(0, ZS - 1)]
    pltpu.make_async_copy(sent, sent, zsend_sem).wait()


def local(energies, sample_counts, state_leg, bin_index):
    hbm = pl.BlockSpec(memory_space=pl.ANY)
    vmem = pl.BlockSpec(memory_space=pltpu.VMEM)
    f32 = jnp.float32
    dma = pltpu.SemaphoreType.DMA
    rdf, leg_free = pl.pallas_call(
        kernel,
        out_shape=(
            jax.ShapeDtypeStruct((OWN, LANES), f32),
            jax.ShapeDtypeStruct((1, LANES), f32),
        ),
        in_specs=[hbm, vmem, vmem, hbm],
        out_specs=(vmem, vmem),
        scratch_shapes=[
            pltpu.VMEM((ROWS, COLS), f32),
            pltpu.VMEM((TYPES, PAIRS, COLS), jnp.int32),
            pltpu.VMEM((TYPES * BINS, COLS), jnp.bfloat16),
            pltpu.VMEM((ROWS, COLS), jnp.bfloat16),
            pltpu.VMEM((ROWS, LANES), f32),
            pltpu.VMEM((BLOCKS, LANES), f32),
            pltpu.VMEM((BLOCKS, LANES), f32),
            pltpu.VMEM((BLOCKS, LANES), f32),
            pltpu.VMEM((ITERS + 1, YS, BLOCKS, LANES), f32),
            pltpu.VMEM((ITERS, FS, 1, LANES), f32),
            pltpu.VMEM((YS, 2, LANES), f32),
            pltpu.VMEM((ZS, XS, 2, OWN, LANES), f32),
            pltpu.VMEM((ZS, XS, OWN, LANES), f32),
            pltpu.VMEM((ZS, XS, OWN, LANES), f32),
            pltpu.VMEM((ZS, XS - 1, OWN, LANES), f32),
            pltpu.VMEM((ZS, OWN, LANES), f32),
            pltpu.VMEM((ZS, OWN, LANES), f32),
            dma((PARTS,)),
            dma,
            dma((ITERS + 1,)),
            dma((ITERS + 1,)),
            dma((ITERS,)),
            dma((ITERS,)),
            dma,
            dma,
            dma,
            dma((ZS,)),
            dma,
            dma((ZS,)),
            dma,
            dma,
        ],
        compiler_params=pltpu.CompilerParams(
            collective_id=0, has_side_effects=True, vmem_limit_bytes=56 * 2**20
        ),
        name="reweight",
    )(
        energies,
        sample_counts.reshape(1, LANES),
        state_leg.reshape(1, LANES),
        jnp.transpose(bin_index, (1, 2, 0)),
    )
    return rdf, leg_free.reshape(LANES)


def solution(mesh):
    placed = (P("state", "frame"), P("state"), P("state"), P("frame", None, None))
    return jax.shard_map(
        local,
        mesh=mesh,
        in_specs=placed,
        out_specs=(P("frame", "state"), P("state")),
        check_vma=False,
    )
```

```python
import functools

import jax
import jax.numpy as jnp
from jax import lax
from jax.experimental import pallas as pl
from jax.experimental.pallas import tpu as pltpu
from jax.sharding import PartitionSpec as P

BINS = 256
TYPES = 6
PAIRS = 8
LEGS = 8
ITERS = 2
YS = 4
XS = 4
ZS = 8
FS = XS * ZS * 2
LANES = 128
ROWS = 128
COLS = 8192
BLOCKS = COLS // LANES
OWN = TYPES * BINS // FS
PARTS = 4
GROUPS = ROWS // 8
WIDE = 256
LOG2E = 1.4426950408889634
LN2 = 0.6931471805599453
UNROLL = 4
FAR = 3
MESH = pl.DeviceIdType.MESH


def eye():
    shape = (ROWS, LANES)
    return lax.broadcasted_iota(jnp.int32, shape, 0) == lax.broadcasted_iota(jnp.int32, shape, 1)


def to_col(row):
    return jnp.sum(jnp.where(eye(), jnp.broadcast_to(row, (ROWS, LANES)), 0.0), axis=1, keepdims=True)


def to_row(col):
    return jnp.sum(jnp.where(eye(), jnp.broadcast_to(col, (ROWS, LANES)), 0.0), axis=0, keepdims=True)


def place(row):
    group, rest = divmod(row, 2 * OWN)
    x, z = divmod(group, ZS)
    return z * (XS * 2 * OWN) + x * 2 * OWN + rest


def count_block(bins, counts, block):
    cols = pl.ds(pl.multiple_of(block * WIDE, WIDE), WIDE)
    iota = lax.broadcasted_iota(jnp.int32, (16, WIDE), 0)
    for t in range(TYPES):
        rows = bins[t, :, cols]
        low = rows & 15
        one = jnp.left_shift(1, (rows >> 4) * 2)
        even = odd = None
        for group in ((0, 1, 2), (3, 4, 5), (6, 7)):
            word = None
            for p in group:
                hot = jnp.where(low[p : p + 1] == iota, one[p : p + 1], 0)
                word = hot if word is None else word + hot
            a = word & 0x33333333
            b = lax.shift_right_logical(word, 2) & 0x33333333
            even = a if even is None else even + a
            odd = b if odd is None else odd + b
        for half, nibbles in ((0, even), (16, odd)):
            for q in range(0, 8, 2):
                v = lax.shift_right_logical(nibbles, 4 * q) if q else nibbles
                if q < 6:
                    v = v & 255
                v = v.astype(jnp.float32).astype(jnp.bfloat16)
                upper = (v + jnp.bfloat16(2048)) - jnp.bfloat16(2048)
                base = t * BINS + 32 * q + half
                counts[pl.ds(place(base), 16), cols] = v - upper
                counts[pl.ds(place(base + 32), 16), cols] = upper * jnp.bfloat16(0.0625)


def folded(value, op):
    parts = [value[8 * g : 8 * g + 8] for g in range(GROUPS)]
    while len(parts) > 1:
        parts = [op(parts[i], parts[i + 1]) for i in range(0, len(parts), 2)]
    return parts[0]


def kernel(
    e_hbm, n_ref, leg_ref, bins_hbm, out_ref,
    energies, bins, counts, weights, fold, mbuf, dbuf,
    ybuf, fbuf, legbuf, part, crecv, xsend, xrecv, drecv, zsend, zrecv,
    e_sem, bins_sem, ysend_sem, yrecv_sem, fsend_sem, frecv_sem, legsend_sem, legrecv_sem,
    csend_sem, crecv_sem, xsend_sem, xrecv_sem, dsend_sem, drecv_sem, zsend_sem, zrecv_sem,
):
    y = lax.axis_index("state")
    f = lax.axis_index("frame")
    core = lax.rem(f, 2)
    z = lax.rem(lax.div(f, 2), ZS)
    x = lax.div(f, 2 * ZS)
    width = COLS // PARTS

    loads = [
        pltpu.make_async_copy(
            e_hbm.at[:, pl.ds(i * width, width)], energies.at[:, pl.ds(i * width, width)], e_sem.at[i]
        )
        for i in range(PARTS)
    ]
    for load in loads:
        load.start()
    bins_load = pltpu.make_async_copy(bins_hbm, bins, bins_sem)
    bins_load.start()

    barrier = pltpu.get_barrier_semaphore()

    def greet(d, _):
        pl.semaphore_signal(barrier, inc=1, device_id=(y, lax.rem(f + d, FS)), device_id_type=MESH)
        return 0

    for d in range(1, YS):
        pl.semaphore_signal(barrier, inc=1, device_id=(lax.rem(y + d, YS), f), device_id_type=MESH)
    lax.fori_loop(1, FS, greet, 0)

    def count(first, last):
        def body(b, _):
            count_block(bins, counts, b)
            return 0

        lax.fori_loop(first, last, body, 0)

    def wide(col):
        return jnp.broadcast_to(col, (ROWS, LANES))

    def at(j):
        return pl.ds(pl.multiple_of(j * LANES, LANES), LANES)

    def eight(j):
        return pl.ds(pl.multiple_of(j * 8, 8), 8)

    def unfold(op):
        return functools.reduce(op, [fold[pl.ds(r, BLOCKS, stride=8), :] for r in range(8)])

    def scale_and_peak(terms, first, last):
        def body(j, _):
            e = energies[:, at(j)] * -LOG2E
            energies[:, at(j)] = e
            fold[eight(j), :] = folded(terms + e, jnp.maximum)
            return 0

        lax.fori_loop(first, last, body, 0, unroll=UNROLL)

    def peak(terms):
        def body(j, _):
            fold[eight(j), :] = folded(terms + energies[:, at(j)], jnp.maximum)
            return 0

        lax.fori_loop(0, BLOCKS, body, 0, unroll=UNROLL)

    def state_sum(terms, stage):
        mbuf[...] = unfold(jnp.maximum)

        def body(j, _):
            scores = (terms + energies[:, at(j)]) - mbuf[pl.ds(j, 1), :]
            fold[eight(j), :] = folded(jnp.exp2(scores), jnp.add)
            return 0

        lax.fori_loop(0, BLOCKS, body, 0, unroll=UNROLL)
        ybuf[stage, y] = mbuf[...] + jnp.log(unfold(jnp.add)) * LOG2E

    def y_send(stage):
        for d in (2, 1, 3):
            pltpu.make_async_remote_copy(
                src_ref=ybuf.at[stage, y], dst_ref=ybuf.at[stage, y],
                send_sem=ysend_sem.at[stage], recv_sem=yrecv_sem.at[stage],
                device_id=(lax.rem(y + d, YS), f), device_id_type=MESH,
            ).start()

    def y_finish(stage):
        got = ybuf.at[stage, pl.ds(0, YS - 1)]
        pltpu.make_async_copy(got, got, yrecv_sem.at[stage]).wait()
        parts = [ybuf[stage, k] for k in range(YS)]
        largest = functools.reduce(jnp.maximum, parts)
        total = functools.reduce(jnp.add, [jnp.exp2(part - largest) for part in parts])
        dbuf[...] = largest + jnp.log(total) * LOG2E

    def frame_sum(stage):
        def greatest(j, most):
            return jnp.maximum(most, energies[:, at(j)] - dbuf[pl.ds(j, 1), :])

        most = lax.fori_loop(
            0, BLOCKS, greatest, jnp.full((ROWS, LANES), -jnp.inf, jnp.float32), unroll=UNROLL
        )
        most = jnp.max(most, axis=1, keepdims=True)
        shift = wide(most)

        def add(j, total):
            return total + jnp.exp2((energies[:, at(j)] - dbuf[pl.ds(j, 1), :]) - shift)

        total = lax.fori_loop(0, BLOCKS, add, jnp.zeros((ROWS, LANES), jnp.float32), unroll=UNROLL)
        total = jnp.sum(total, axis=1, keepdims=True)
        fbuf[stage, f] = to_row(most) + jnp.log(to_row(total)) * LOG2E

    def hops(k):
        dx, dz, dc = k
        return min(dx, XS - dx) + min(dz, ZS - dz) + 0.5 * dc

    frame_partners = sorted(
        [(dx, dz, dc) for dx in range(XS) for dz in range(ZS) for dc in range(2)], key=hops, reverse=True
    )[:-1]
    x_at = [lax.rem(x + d, XS) * (2 * ZS) for d in range(XS)]
    z_at = [lax.rem(z + d, ZS) * 2 for d in range(ZS)]
    c_at = [core, 1 - core]

    def f_send(stage):
        for dx, dz, dc in frame_partners:
            pltpu.make_async_remote_copy(
                src_ref=fbuf.at[stage, f], dst_ref=fbuf.at[stage, f],
                send_sem=fsend_sem.at[stage], recv_sem=frecv_sem.at[stage],
                device_id=(y, x_at[dx] + z_at[dz] + c_at[dc]), device_id_type=MESH,
            ).start()

    def f_finish(stage):
        got = fbuf.at[stage, pl.ds(0, FS - 1)]
        pltpu.make_async_copy(got, got, frecv_sem.at[stage]).wait()
        parts = fbuf[stage]
        largest = jnp.max(parts, axis=0)
        return -(largest + jnp.log(jnp.sum(jnp.exp2(parts - largest[None]), axis=0)) * LOG2E)

    log_counts = jnp.log(n_ref[...].astype(jnp.float32)) * LOG2E
    terms = wide(to_col(log_counts))
    for i in range(PARTS):
        loads[i].wait()
        scale_and_peak(terms, i * BLOCKS // PARTS, (i + 1) * BLOCKS // PARTS)
    state_sum(terms, 0)
    bins_load.wait()
    blocks = COLS // WIDE
    pl.semaphore_wait(barrier, YS - 1 + FS - 1)
    y_send(0)
    count(0, blocks // 4)
    y_finish(0)
    frame_sum(0)
    f_send(0)
    count(blocks // 4, 3 * blocks // 4)
    free = f_finish(0)

    terms = wide(to_col(log_counts + free))
    peak(terms)
    state_sum(terms, 1)
    y_send(1)
    count(3 * blocks // 4, blocks)
    y_finish(1)
    frame_sum(1)
    f_send(1)
    free = f_finish(1)

    terms = wide(to_col(log_counts + free))
    peak(terms)
    state_sum(terms, 2)
    y_send(2)
    free_col = to_col(free)
    factors = wide(free_col)
    y_finish(2)

    def weigh(j, _):
        value = jnp.exp2((factors + energies[:, at(j)]) - dbuf[pl.ds(j, 1), :])
        weights[:, at(j)] = value.astype(jnp.bfloat16)
        return 0

    lax.fori_loop(0, BLOCKS, weigh, 0, unroll=UNROLL)

    def offset(s):
        return 4 + (1 - 2 * lax.rem(s, 2)) * lax.div(s + 1, 2)

    def core_copy(s):
        other = 1 - core
        return pltpu.make_async_remote_copy(
            src_ref=part.at[s, :, other], dst_ref=crecv.at[s],
            send_sem=csend_sem, recv_sem=crecv_sem.at[s],
            device_id=(y, f + 1 - 2 * core), device_id_type=MESH,
        )

    def x_copy(s, d):
        to = lax.rem(x + d, XS)
        return pltpu.make_async_remote_copy(
            src_ref=xsend.at[s, to], dst_ref=xrecv.at[s, d - 1],
            send_sem=xsend_sem, recv_sem=xrecv_sem.at[s],
            device_id=(y, to * (2 * ZS) + z * 2 + core), device_id_type=MESH,
        )

    def near_copy(s, d):
        to = lax.rem(x + d, XS)
        to_z = lax.rem(z + offset(s), ZS)
        return pltpu.make_async_remote_copy(
            src_ref=xsend.at[s, to], dst_ref=drecv.at[s - FAR, d],
            send_sem=dsend_sem, recv_sem=drecv_sem.at[s - FAR],
            device_id=(y, to * (2 * ZS) + to_z * 2 + core), device_id_type=MESH,
        )

    def z_copy(s):
        to = lax.rem(z + offset(s), ZS)
        return pltpu.make_async_remote_copy(
            src_ref=zsend.at[s], dst_ref=zrecv.at[s],
            send_sem=zsend_sem, recv_sem=zrecv_sem,
            device_id=(y, x * (2 * ZS) + to * 2 + core), device_id_type=MESH,
        )

    def core_post(s):
        pltpu.make_async_copy(crecv.at[s], crecv.at[s], crecv_sem.at[s]).wait()
        xsend[s] = part[s, :, core] + crecv[s]

    def far_post(s):
        core_post(s)
        for d in (2, 1, 3):
            x_copy(s, d).start()

    def near_post(s):
        core_post(s)
        for d in (2, 1, 3, 0):
            near_copy(s, d).start()

    def x_post(s):
        pltpu.make_async_copy(xrecv.at[s], xrecv.at[s], xrecv_sem.at[s]).wait()
        zsend[s] = (xsend[s, x] + xrecv[s, 0]) + (xrecv[s, 1] + xrecv[s, 2])
        z_copy(s).start()

    lag = 5

    def step(s, _):
        rows = pl.ds(pl.multiple_of(lax.rem(z + offset(s), ZS) * (XS * 2 * OWN), 32), XS * 2 * OWN)
        result = lax.dot_general(
            counts[rows, :], weights[...], (((1,), (1,)), ((), ())), preferred_element_type=jnp.float32
        )
        part[s] = result.reshape(XS, 2, OWN, LANES)
        core_copy(s).start()

        @pl.when(jnp.logical_and(s >= 1, s <= FAR))
        def _():
            far_post(s - 1)

        @pl.when(s > FAR)
        def _():
            near_post(s - 1)

        @pl.when(s >= lag)
        def _():
            x_post(s - lag)

        return 0

    lax.fori_loop(0, ZS, step, 0)
    last = ZS - 1
    core_post(last)
    for d in (2, 1, 3):
        near_copy(last, d).start()

    leg_col = to_col(leg_ref[...].astype(jnp.float32))
    lane = lax.broadcasted_iota(jnp.int32, (ROWS, LANES), 1).astype(jnp.float32)
    table = (wide(leg_col) == lane).astype(jnp.float32)
    legbuf[y, 0:1] = jnp.sum(table * factors, axis=0, keepdims=True)
    legbuf[y, 1:2] = jnp.sum(table, axis=0, keepdims=True)
    for d in (2, 1, 3):
        pltpu.make_async_remote_copy(
            src_ref=legbuf.at[y], dst_ref=legbuf.at[y],
            send_sem=legsend_sem, recv_sem=legrecv_sem,
            device_id=(lax.rem(y + d, YS), f), device_id_type=MESH,
        ).start()
    got = zrecv.at[pl.ds(0, FAR)]
    pltpu.make_async_copy(got, got, zrecv_sem).wait()
    total = xsend[last, x]
    for s in range(FAR):
        total = total + zrecv[s]
    for s in range(FAR, last):
        got = drecv.at[s - FAR]
        pltpu.make_async_copy(got, got, drecv_sem.at[s - FAR]).wait()
        for d in range(XS):
            total = total + drecv[s - FAR, d]
    got = drecv.at[last - FAR, pl.ds(1, XS - 1)]
    pltpu.make_async_copy(got, got, drecv_sem.at[last - FAR]).wait()
    for d in range(1, XS):
        total = total + drecv[last - FAR, d]
    out_ref[0:OWN, :] = total * (BINS / PAIRS)
    got = legbuf.at[pl.ds(0, YS - 1)]
    pltpu.make_async_copy(got, got, legrecv_sem).wait()
    legs = (legbuf[0] + legbuf[1]) + (legbuf[2] + legbuf[3])
    leg_mean = legs[0:1] / jnp.maximum(legs[1:2], 1.0)
    own_mean = jnp.sum(table * jnp.broadcast_to(leg_mean, (ROWS, LANES)), axis=1, keepdims=True)
    out_ref[OWN : OWN + 8, :] = jnp.broadcast_to(to_row((free_col - own_mean) * LN2), (8, LANES))

    for stage in range(ITERS + 1):
        sent = ybuf.at[stage, pl.ds(0, YS - 1)]
        pltpu.make_async_copy(sent, sent, ysend_sem.at[stage]).wait()
    for stage in range(ITERS):
        sent = fbuf.at[stage, pl.ds(0, FS - 1)]
        pltpu.make_async_copy(sent, sent, fsend_sem.at[stage]).wait()
    sent = legbuf.at[pl.ds(0, YS - 1)]
    pltpu.make_async_copy(sent, sent, legsend_sem).wait()
    pltpu.make_async_copy(crecv, crecv, csend_sem).wait()
    pltpu.make_async_copy(xrecv, xrecv, xsend_sem).wait()
    sent = drecv.at[pl.ds(0, last - FAR)]
    pltpu.make_async_copy(sent, sent, dsend_sem).wait()
    sent = drecv.at[last - FAR, pl.ds(1, XS - 1)]
    pltpu.make_async_copy(sent, sent, dsend_sem).wait()
    sent = zrecv.at[pl.ds(0, FAR)]
    pltpu.make_async_copy(sent, sent, zsend_sem).wait()


def split(both_ref, rdf_ref, leg_ref):
    rdf_ref[...] = both_ref[0:OWN, :]
    leg_ref[...] = both_ref[OWN : OWN + 1, :]


def local(energies, sample_counts, state_leg, bin_index):
    hbm = pl.BlockSpec(memory_space=pl.ANY)
    vmem = pl.BlockSpec(memory_space=pltpu.VMEM)
    f32 = jnp.float32
    dma = pltpu.SemaphoreType.DMA
    both = pl.pallas_call(
        kernel,
        out_shape=jax.ShapeDtypeStruct((OWN + 8, LANES), f32),
        in_specs=[hbm, vmem, vmem, hbm],
        out_specs=vmem,
        scratch_shapes=[
            pltpu.VMEM((ROWS, COLS), f32),
            pltpu.VMEM((TYPES, PAIRS, COLS), jnp.int32),
            pltpu.VMEM((TYPES * BINS, COLS), jnp.bfloat16),
            pltpu.VMEM((ROWS, COLS), jnp.bfloat16),
            pltpu.VMEM((BLOCKS * 8, LANES), f32),
            pltpu.VMEM((BLOCKS, LANES), f32),
            pltpu.VMEM((BLOCKS, LANES), f32),
            pltpu.VMEM((ITERS + 1, YS, BLOCKS, LANES), f32),
            pltpu.VMEM((ITERS, FS, 1, LANES), f32),
            pltpu.VMEM((YS, 2, LANES), f32),
            pltpu.VMEM((ZS, XS, 2, OWN, LANES), f32),
            pltpu.VMEM((ZS, XS, OWN, LANES), f32),
            pltpu.VMEM((ZS, XS, OWN, LANES), f32),
            pltpu.VMEM((FAR, XS - 1, OWN, LANES), f32),
            pltpu.VMEM((ZS - FAR, XS, OWN, LANES), f32),
            pltpu.VMEM((FAR, OWN, LANES), f32),
            pltpu.VMEM((FAR, OWN, LANES), f32),
            dma((PARTS,)),
            dma,
            dma((ITERS + 1,)),
            dma((ITERS + 1,)),
            dma((ITERS,)),
            dma((ITERS,)),
            dma,
            dma,
            dma,
            dma((ZS,)),
            dma,
            dma((FAR,)),
            dma,
            dma((ZS - FAR,)),
            dma,
            dma,
        ],
        compiler_params=pltpu.CompilerParams(
            collective_id=0, has_side_effects=True, vmem_limit_bytes=56 * 2**20
        ),
        name="reweight",
    )(
        energies,
        sample_counts.reshape(1, LANES),
        state_leg.reshape(1, LANES),
        jnp.transpose(bin_index, (1, 2, 0)),
    )
    rdf, leg_free = pl.pallas_call(
        split,
        out_shape=(jax.ShapeDtypeStruct((OWN, LANES), f32), jax.ShapeDtypeStruct((1, LANES), f32)),
        in_specs=[vmem],
        out_specs=(vmem, vmem),
        name="split",
    )(both)
    return rdf, leg_free.reshape(LANES)


def solution(mesh):
    placed = (P("state", "frame"), P("state"), P("state"), P("frame", None, None))
    return jax.shard_map(
        local,
        mesh=mesh,
        in_specs=placed,
        out_specs=(P("frame", "state"), P("state")),
        check_vma=False,
    )
```

```python
import functools

import jax
import jax.numpy as jnp
from jax import lax
from jax.experimental import pallas as pl
from jax.experimental.pallas import tpu as pltpu
from jax.sharding import PartitionSpec as P

BINS = 256
TYPES = 6
PAIRS = 8
LEGS = 8
ITERS = 2
YS = 4
XS = 4
ZS = 8
FS = XS * ZS * 2
LANES = 128
ROWS = 128
COLS = 8192
BLOCKS = COLS // LANES
OWN = TYPES * BINS // FS
PARTS = 4
GROUPS = ROWS // 8
WIDE = 256
LOG2E = 1.4426950408889634
LN2 = 0.6931471805599453
UNROLL = 4
HALF = BLOCKS // 2
SPAN = 8
FAR = 3
MESH = pl.DeviceIdType.MESH


def eye():
    shape = (ROWS, LANES)
    return lax.broadcasted_iota(jnp.int32, shape, 0) == lax.broadcasted_iota(jnp.int32, shape, 1)


def to_col(row):
    return jnp.sum(jnp.where(eye(), jnp.broadcast_to(row, (ROWS, LANES)), 0.0), axis=1, keepdims=True)


def to_row(col):
    return jnp.sum(jnp.where(eye(), jnp.broadcast_to(col, (ROWS, LANES)), 0.0), axis=0, keepdims=True)


def place(row):
    group, rest = divmod(row, 2 * OWN)
    x, z = divmod(group, ZS)
    return z * (XS * 2 * OWN) + x * 2 * OWN + rest


def count_block(bins, counts, block):
    cols = pl.ds(pl.multiple_of(block * WIDE, WIDE), WIDE)
    iota = lax.broadcasted_iota(jnp.int32, (16, WIDE), 0)
    for t in range(TYPES):
        rows = bins[t, :, cols]
        low = rows & 15
        one = jnp.left_shift(1, (rows >> 4) * 2)
        even = odd = None
        for group in ((0, 1, 2), (3, 4, 5), (6, 7)):
            word = None
            for p in group:
                hot = jnp.where(low[p : p + 1] == iota, one[p : p + 1], 0)
                word = hot if word is None else word + hot
            a = word & 0x33333333
            b = lax.shift_right_logical(word, 2) & 0x33333333
            even = a if even is None else even + a
            odd = b if odd is None else odd + b
        for half, nibbles in ((0, even), (16, odd)):
            for q in range(0, 8, 2):
                v = lax.shift_right_logical(nibbles, 4 * q) if q else nibbles
                if q < 6:
                    v = v & 255
                v = v.astype(jnp.float32).astype(jnp.bfloat16)
                upper = (v + jnp.bfloat16(2048)) - jnp.bfloat16(2048)
                base = t * BINS + 32 * q + half
                counts[pl.ds(place(base), 16), cols] = v - upper
                counts[pl.ds(place(base + 32), 16), cols] = upper * jnp.bfloat16(0.0625)


def online(parts):
    largest = functools.reduce(jnp.maximum, parts)
    return largest, functools.reduce(jnp.add, [jnp.exp2(part - largest) for part in parts])


def merged(pairs):
    largest = functools.reduce(jnp.maximum, [m for m, _ in pairs])
    return largest, functools.reduce(jnp.add, [s * jnp.exp2(m - largest) for m, s in pairs])


def kernel(
    e_hbm, n_hbm, leg_hbm, bins_hbm, out_ref,
    energies, n_ref, leg_ref, bins, counts, weights, terms, state_max, state_sum, frame_max, frame_sum, dbuf,
    ybuf, fbuf, legbuf, part, crecv, xsend, xrecv, drecv, zsend, zrecv,
    e_sem, small_sem, bins_sem, z_ready, xc_ready, ysend_sem, yrecv_sem, fsend_sem, frecv_sem, legsend_sem, legrecv_sem,
    csend_sem, crecv_sem, xsend_sem, xrecv_sem, dsend_sem, drecv_sem, zsend_sem, zrecv_sem,
):
    y = lax.axis_index("state")
    f = lax.axis_index("frame")
    core = lax.rem(f, 2)
    z = lax.rem(lax.div(f, 2), ZS)
    x = lax.div(f, 2 * ZS)
    width = COLS // PARTS
    x_at = [lax.rem(x + d, XS) * (2 * ZS) for d in range(XS)]
    z_at = [lax.rem(z + d, ZS) * 2 for d in range(ZS)]
    c_at = [core, 1 - core]
    y_near = [(lax.rem(y + d, YS), f) for d in (2, 1, 3)]
    z_near = [(y, x_at[0] + z_at[d] + core) for d in (2, 6, 1, 7)]
    xc_near = [
        (y, x_at[dx] + z_at[0] + c_at[dc]) for dx, dc in ((2, 1), (2, 0), (1, 1), (3, 1), (1, 0), (3, 0), (0, 1))
    ]

    barrier = pltpu.get_barrier_semaphore()
    for device in y_near + z_near + xc_near:
        pl.semaphore_signal(barrier, inc=1, device_id=device, device_id_type=MESH)

    n_load = pltpu.make_async_copy(n_hbm, n_ref, small_sem.at[0])
    n_load.start()
    loads = [
        pltpu.make_async_copy(
            e_hbm.at[:, pl.ds(i * width, width)], energies.at[:, pl.ds(i * width, width)], e_sem.at[i]
        )
        for i in range(PARTS)
    ]
    for load in loads:
        load.start()
    bins_load = pltpu.make_async_copy(bins_hbm, bins, bins_sem)
    bins_load.start()
    leg_load = pltpu.make_async_copy(leg_hbm, leg_ref, small_sem.at[1])
    leg_load.start()

    def count(first, last):
        def body(b, _):
            count_block(bins, counts, b)
            return 0

        lax.fori_loop(first, last, body, 0)

    def wide(col):
        return jnp.broadcast_to(col, (ROWS, LANES))

    def at(j):
        return pl.ds(pl.multiple_of(j * LANES, LANES), LANES)

    def eight(j):
        return pl.ds(pl.multiple_of(j * 8, 8), 8)

    def state_pass(first, last, scale=False):
        def body(k, _):
            for u in range(SPAN):
                j = k * SPAN + u
                pairs = []
                for h in range(2):
                    scores = []
                    for g in range(h * GROUPS // 2, (h + 1) * GROUPS // 2):
                        rows = pl.ds(8 * g, 8)
                        e = energies[rows, at(j)]
                        if scale:
                            e = e * -LOG2E
                            energies[rows, at(j)] = e
                        scores.append(terms[rows, :] + e)
                    pairs.append(online(scores))
                state_max[eight(j), :], state_sum[eight(j), :] = merged(pairs)
            return 0

        lax.fori_loop(first // SPAN, last // SPAN, body, 0)

    def y_send(stage, half):
        rows = [pl.ds(half * HALF * 8 + r, HALF, stride=8) for r in range(8)]
        largest, total = merged([(state_max[r, :], state_sum[r, :]) for r in rows])
        ybuf[stage, half, y] = largest + jnp.log(total) * LOG2E
        for device in y_near:
            pltpu.make_async_remote_copy(
                src_ref=ybuf.at[stage, half, y], dst_ref=ybuf.at[stage, half, y],
                send_sem=ysend_sem.at[stage, half], recv_sem=yrecv_sem.at[stage, half],
                device_id=device, device_id_type=MESH,
            ).start()

    def y_finish(stage, half):
        got = ybuf.at[stage, half, pl.ds(0, YS - 1)]
        pltpu.make_async_copy(got, got, yrecv_sem.at[stage, half]).wait()
        largest, total = online([ybuf[stage, half, k] for k in range(YS)])
        dbuf[pl.ds(half * HALF, HALF), :] = largest + jnp.log(total) * LOG2E

    def frame_pass(half):
        def body(b, _):
            divisors = [dbuf[pl.ds(b * SPAN + u, 1), :] for u in range(SPAN)]
            for g in range(GROUPS):
                rows = pl.ds(8 * g, 8)
                frame_max[b, rows, :], frame_sum[b, rows, :] = online(
                    [energies[rows, at(b * SPAN + u)] - divisors[u] for u in range(SPAN)]
                )
            return 0

        lax.fori_loop(half * HALF // SPAN, (half + 1) * HALF // SPAN, body, 0)

    frame_partners = sorted(
        [(dx, dz, dc) for dx in range(XS) for dz in range(ZS) for dc in range(2)],
        key=lambda k: min(k[0], XS - k[0]) + min(k[1], ZS - k[1]) + 0.5 * k[2],
        reverse=True,
    )[:-1]

    def f_send(stage):
        largest, total = merged([(frame_max[b], frame_sum[b]) for b in range(BLOCKS // SPAN)])
        most = jnp.max(largest, axis=1, keepdims=True)
        total = jnp.sum(total * jnp.exp2(largest - most), axis=1, keepdims=True)
        fbuf[stage, f] = to_row(most) + jnp.log(to_row(total)) * LOG2E
        for dx, dz, dc in frame_partners:
            pltpu.make_async_remote_copy(
                src_ref=fbuf.at[stage, f], dst_ref=fbuf.at[stage, f],
                send_sem=fsend_sem.at[stage], recv_sem=frecv_sem.at[stage],
                device_id=(y, x_at[dx] + z_at[dz] + c_at[dc]), device_id_type=MESH,
            ).start()

    def f_finish(stage):
        got = fbuf.at[stage, pl.ds(0, FS - 1)]
        pltpu.make_async_copy(got, got, frecv_sem.at[stage]).wait()
        parts = fbuf[stage]
        largest = jnp.max(parts, axis=0)
        return -(largest + jnp.log(jnp.sum(jnp.exp2(parts - largest[None]), axis=0)) * LOG2E)

    n_load.wait()
    log_counts = jnp.log(n_ref[...].astype(jnp.float32)) * LOG2E
    terms[...] = wide(to_col(log_counts))
    share = BLOCKS // PARTS
    loads[0].wait()
    state_pass(0, share, scale=True)
    loads[1].wait()
    state_pass(share, 2 * share, scale=True)
    pl.semaphore_wait(barrier, len(y_near + z_near + xc_near))
    for device in z_near[:2]:
        pl.semaphore_signal(z_ready, inc=1, device_id=device, device_id_type=MESH)
    y_send(0, 0)
    loads[2].wait()
    state_pass(2 * share, 3 * share, scale=True)
    loads[3].wait()
    state_pass(3 * share, 4 * share, scale=True)
    y_send(0, 1)
    bins_load.wait()
    count(0, 6)
    pl.semaphore_wait(z_ready, 2)
    for device in xc_near:
        pl.semaphore_signal(xc_ready, inc=1, device_id=device, device_id_type=MESH)
    y_finish(0, 0)
    frame_pass(0)
    y_finish(0, 1)
    frame_pass(1)
    pl.semaphore_wait(xc_ready, len(xc_near))
    f_send(0)
    count(6, 18)
    free = f_finish(0)

    terms[...] = wide(to_col(log_counts + free))
    state_pass(0, HALF)
    y_send(1, 0)
    state_pass(HALF, BLOCKS)
    y_send(1, 1)
    count(18, 24)
    y_finish(1, 0)
    frame_pass(0)
    y_finish(1, 1)
    frame_pass(1)
    f_send(1)
    count(24, COLS // WIDE)
    free = f_finish(1)

    terms[...] = wide(to_col(log_counts + free))
    state_pass(0, HALF)
    y_send(2, 0)
    state_pass(HALF, BLOCKS)
    y_send(2, 1)
    free_col = to_col(free)
    factors = wide(free_col)
    terms[...] = factors

    def weigh(j, _):
        value = jnp.exp2((terms[...] + energies[:, at(j)]) - dbuf[pl.ds(j, 1), :])
        weights[:, at(j)] = value.astype(jnp.bfloat16)
        return 0

    for half in range(2):
        y_finish(2, half)
        lax.fori_loop(half * HALF, (half + 1) * HALF, weigh, 0, unroll=SPAN)

    def offset(s):
        return 4 + (1 - 2 * lax.rem(s, 2)) * lax.div(s + 1, 2)

    def core_copy(s):
        other = 1 - core
        return pltpu.make_async_remote_copy(
            src_ref=part.at[s, :, other], dst_ref=crecv.at[s],
            send_sem=csend_sem, recv_sem=crecv_sem.at[s],
            device_id=(y, f + 1 - 2 * core), device_id_type=MESH,
        )

    def x_copy(s, d):
        to = lax.rem(x + d, XS)
        return pltpu.make_async_remote_copy(
            src_ref=xsend.at[s, to], dst_ref=xrecv.at[s, d - 1],
            send_sem=xsend_sem, recv_sem=xrecv_sem.at[s],
            device_id=(y, to * (2 * ZS) + z * 2 + core), device_id_type=MESH,
        )

    def near_copy(s, d):
        to = lax.rem(x + d, XS)
        to_z = lax.rem(z + offset(s), ZS)
        return pltpu.make_async_remote_copy(
            src_ref=xsend.at[s, to], dst_ref=drecv.at[s - FAR, d],
            send_sem=dsend_sem, recv_sem=drecv_sem.at[s - FAR],
            device_id=(y, to * (2 * ZS) + to_z * 2 + core), device_id_type=MESH,
        )

    def z_copy(s):
        to = lax.rem(z + offset(s), ZS)
        return pltpu.make_async_remote_copy(
            src_ref=zsend.at[s], dst_ref=zrecv.at[s],
            send_sem=zsend_sem, recv_sem=zrecv_sem,
            device_id=(y, x * (2 * ZS) + to * 2 + core), device_id_type=MESH,
        )

    def core_post(s):
        pltpu.make_async_copy(crecv.at[s], crecv.at[s], crecv_sem.at[s]).wait()
        xsend[s] = part[s, :, core] + crecv[s]

    def far_post(s):
        core_post(s)
        for d in (2, 1, 3):
            x_copy(s, d).start()

    def near_post(s):
        core_post(s)
        for d in (2, 1, 3, 0):
            near_copy(s, d).start()

    def x_post(s):
        pltpu.make_async_copy(xrecv.at[s], xrecv.at[s], xrecv_sem.at[s]).wait()
        zsend[s] = (xsend[s, x] + xrecv[s, 0]) + (xrecv[s, 1] + xrecv[s, 2])
        z_copy(s).start()

    lag = 5

    def step(s, _):
        rows = pl.ds(pl.multiple_of(lax.rem(z + offset(s), ZS) * (XS * 2 * OWN), 32), XS * 2 * OWN)
        result = lax.dot_general(
            counts[rows, :], weights[...], (((1,), (1,)), ((), ())), preferred_element_type=jnp.float32
        )
        part[s] = result.reshape(XS, 2, OWN, LANES)
        core_copy(s).start()

        @pl.when(jnp.logical_and(s >= 1, s <= FAR))
        def _():
            far_post(s - 1)

        @pl.when(s > FAR)
        def _():
            near_post(s - 1)

        @pl.when(s >= lag)
        def _():
            x_post(s - lag)

        return 0

    lax.fori_loop(0, ZS, step, 0)
    last = ZS - 1
    core_post(last)
    for d in (2, 1, 3):
        near_copy(last, d).start()

    leg_load.wait()
    leg_col = to_col(leg_ref[...].astype(jnp.float32))
    lane = lax.broadcasted_iota(jnp.int32, (ROWS, LANES), 1).astype(jnp.float32)
    table = (wide(leg_col) == lane).astype(jnp.float32)
    legbuf[y, 0:1] = jnp.sum(table * factors, axis=0, keepdims=True)
    legbuf[y, 1:2] = jnp.sum(table, axis=0, keepdims=True)
    for device in y_near:
        pltpu.make_async_remote_copy(
            src_ref=legbuf.at[y], dst_ref=legbuf.at[y],
            send_sem=legsend_sem, recv_sem=legrecv_sem,
            device_id=device, device_id_type=MESH,
        ).start()
    got = zrecv.at[pl.ds(0, FAR)]
    pltpu.make_async_copy(got, got, zrecv_sem).wait()
    total = xsend[last, x]
    for s in range(FAR):
        total = total + zrecv[s]
    for s in range(FAR, last):
        got = drecv.at[s - FAR]
        pltpu.make_async_copy(got, got, drecv_sem.at[s - FAR]).wait()
        for d in range(XS):
            total = total + drecv[s - FAR, d]
    got = drecv.at[last - FAR, pl.ds(1, XS - 1)]
    pltpu.make_async_copy(got, got, drecv_sem.at[last - FAR]).wait()
    for d in range(1, XS):
        total = total + drecv[last - FAR, d]
    out_ref[0:OWN, :] = total * (BINS / PAIRS)
    got = legbuf.at[pl.ds(0, YS - 1)]
    pltpu.make_async_copy(got, got, legrecv_sem).wait()
    legs = (legbuf[0] + legbuf[1]) + (legbuf[2] + legbuf[3])
    leg_mean = legs[0:1] / jnp.maximum(legs[1:2], 1.0)
    own_mean = jnp.sum(table * jnp.broadcast_to(leg_mean, (ROWS, LANES)), axis=1, keepdims=True)
    out_ref[OWN : OWN + 8, :] = jnp.broadcast_to(to_row((free_col - own_mean) * LN2), (8, LANES))

    for stage in range(ITERS + 1):
        for half in range(2):
            sent = ybuf.at[stage, half, pl.ds(0, YS - 1)]
            pltpu.make_async_copy(sent, sent, ysend_sem.at[stage, half]).wait()
    for stage in range(ITERS):
        sent = fbuf.at[stage, pl.ds(0, FS - 1)]
        pltpu.make_async_copy(sent, sent, fsend_sem.at[stage]).wait()
    sent = legbuf.at[pl.ds(0, YS - 1)]
    pltpu.make_async_copy(sent, sent, legsend_sem).wait()
    pltpu.make_async_copy(crecv, crecv, csend_sem).wait()
    pltpu.make_async_copy(xrecv, xrecv, xsend_sem).wait()
    sent = drecv.at[pl.ds(0, last - FAR)]
    pltpu.make_async_copy(sent, sent, dsend_sem).wait()
    sent = drecv.at[last - FAR, pl.ds(1, XS - 1)]
    pltpu.make_async_copy(sent, sent, dsend_sem).wait()
    sent = zrecv.at[pl.ds(0, FAR)]
    pltpu.make_async_copy(sent, sent, zsend_sem).wait()


def split(both_ref, rdf_ref, leg_ref):
    rdf_ref[...] = both_ref[0:OWN, :]
    leg_ref[...] = both_ref[OWN : OWN + 1, :]


def local(energies, sample_counts, state_leg, bin_index):
    hbm = pl.BlockSpec(memory_space=pl.ANY)
    vmem = pl.BlockSpec(memory_space=pltpu.VMEM)
    f32 = jnp.float32
    dma = pltpu.SemaphoreType.DMA
    both = pl.pallas_call(
        kernel,
        out_shape=jax.ShapeDtypeStruct((OWN + 8, LANES), f32),
        in_specs=[hbm] * 4,
        out_specs=vmem,
        scratch_shapes=[
            pltpu.VMEM((ROWS, COLS), f32),
            pltpu.VMEM((1, LANES), jnp.int32),
            pltpu.VMEM((1, LANES), jnp.int32),
            pltpu.VMEM((TYPES, PAIRS, COLS), jnp.int32),
            pltpu.VMEM((TYPES * BINS, COLS), jnp.bfloat16),
            pltpu.VMEM((ROWS, COLS), jnp.bfloat16),
            pltpu.VMEM((ROWS, LANES), f32),
            pltpu.VMEM((BLOCKS * 8, LANES), f32),
            pltpu.VMEM((BLOCKS * 8, LANES), f32),
            pltpu.VMEM((BLOCKS // SPAN, ROWS, LANES), f32),
            pltpu.VMEM((BLOCKS // SPAN, ROWS, LANES), f32),
            pltpu.VMEM((BLOCKS, LANES), f32),
            pltpu.VMEM((ITERS + 1, 2, YS, HALF, LANES), f32),
            pltpu.VMEM((ITERS, FS, 1, LANES), f32),
            pltpu.VMEM((YS, 2, LANES), f32),
            pltpu.VMEM((ZS, XS, 2, OWN, LANES), f32),
            pltpu.VMEM((ZS, XS, OWN, LANES), f32),
            pltpu.VMEM((ZS, XS, OWN, LANES), f32),
            pltpu.VMEM((FAR, XS - 1, OWN, LANES), f32),
            pltpu.VMEM((ZS - FAR, XS, OWN, LANES), f32),
            pltpu.VMEM((FAR, OWN, LANES), f32),
            pltpu.VMEM((FAR, OWN, LANES), f32),
            dma((PARTS,)),
            dma((2,)),
            dma,
            pltpu.SemaphoreType.REGULAR,
            pltpu.SemaphoreType.REGULAR,
            dma((ITERS + 1, 2)),
            dma((ITERS + 1, 2)),
            dma((ITERS,)),
            dma((ITERS,)),
            dma,
            dma,
            dma,
            dma((ZS,)),
            dma,
            dma((FAR,)),
            dma,
            dma((ZS - FAR,)),
            dma,
            dma,
        ],
        compiler_params=pltpu.CompilerParams(
            collective_id=0, has_side_effects=True, vmem_limit_bytes=56 * 2**20
        ),
        name="reweight",
    )(
        energies,
        sample_counts.reshape(1, LANES),
        state_leg.reshape(1, LANES),
        jnp.transpose(bin_index, (1, 2, 0)),
    )
    rdf, leg_free = pl.pallas_call(
        split,
        out_shape=(jax.ShapeDtypeStruct((OWN, LANES), f32), jax.ShapeDtypeStruct((1, LANES), f32)),
        in_specs=[vmem],
        out_specs=(vmem, vmem),
        name="split",
    )(both)
    return rdf, leg_free.reshape(LANES)


def solution(mesh):
    placed = (P("state", "frame"), P("state"), P("state"), P("frame", None, None))
    return jax.shard_map(
        local,
        mesh=mesh,
        in_specs=placed,
        out_specs=(P("frame", "state"), P("state")),
        check_vma=False,
    )
```

```python
import functools

import jax
import jax.numpy as jnp
from jax import lax
from jax.experimental import pallas as pl
from jax.experimental.pallas import tpu as pltpu
from jax.sharding import PartitionSpec as P

BINS = 256
TYPES = 6
PAIRS = 8
LEGS = 8
ITERS = 2
YS = 4
XS = 4
ZS = 8
FS = XS * ZS * 2
LANES = 128
ROWS = 128
COLS = 8192
BLOCKS = COLS // LANES
OWN = TYPES * BINS // FS
PARTS = 4
GROUPS = ROWS // 8
WIDE = 256
LOG2E = 1.4426950408889634
LN2 = 0.6931471805599453
UNROLL = 4
HALF = BLOCKS // 2
SPAN = 8
FAR = 2
MESH = pl.DeviceIdType.MESH


def eye():
    shape = (ROWS, LANES)
    return lax.broadcasted_iota(jnp.int32, shape, 0) == lax.broadcasted_iota(jnp.int32, shape, 1)


def to_col(row):
    return jnp.sum(jnp.where(eye(), jnp.broadcast_to(row, (ROWS, LANES)), 0.0), axis=1, keepdims=True)


def to_row(col):
    return jnp.sum(jnp.where(eye(), jnp.broadcast_to(col, (ROWS, LANES)), 0.0), axis=0, keepdims=True)


def place(row):
    group, rest = divmod(row, 2 * OWN)
    x, z = divmod(group, ZS)
    return z * (XS * 2 * OWN) + x * 2 * OWN + rest


def count_block(bins, counts, block):
    cols = pl.ds(pl.multiple_of(block * WIDE, WIDE), WIDE)
    iota = lax.broadcasted_iota(jnp.int32, (16, WIDE), 0)
    for t in range(TYPES):
        rows = bins[t, :, cols]
        low = rows & 15
        one = jnp.left_shift(1, (rows >> 4) * 2)
        even = odd = None
        for group in ((0, 1, 2), (3, 4, 5), (6, 7)):
            word = None
            for p in group:
                hot = jnp.where(low[p : p + 1] == iota, one[p : p + 1], 0)
                word = hot if word is None else word + hot
            a = word & 0x33333333
            b = lax.shift_right_logical(word, 2) & 0x33333333
            even = a if even is None else even + a
            odd = b if odd is None else odd + b
        for half, nibbles in ((0, even), (16, odd)):
            for q in range(0, 8, 2):
                v = lax.shift_right_logical(nibbles, 4 * q) if q else nibbles
                if q < 6:
                    v = v & 255
                v = v.astype(jnp.float32).astype(jnp.bfloat16)
                upper = (v + jnp.bfloat16(2048)) - jnp.bfloat16(2048)
                base = t * BINS + 32 * q + half
                counts[pl.ds(place(base), 16), cols] = v - upper
                counts[pl.ds(place(base + 32), 16), cols] = upper * jnp.bfloat16(0.0625)


def online(parts):
    largest = functools.reduce(jnp.maximum, parts)
    return largest, functools.reduce(jnp.add, [jnp.exp2(part - largest) for part in parts])


def merged(pairs):
    largest = functools.reduce(jnp.maximum, [m for m, _ in pairs])
    return largest, functools.reduce(jnp.add, [s * jnp.exp2(m - largest) for m, s in pairs])


def kernel(
    e_hbm, n_hbm, leg_hbm, bins_hbm, out_ref,
    energies, n_ref, leg_ref, bins, counts, weights, terms, state_max, state_sum, frame_max, frame_sum, dbuf,
    ybuf, fbuf, legbuf, part, crecv, xsend, xrecv, drecv, lrecv, zsend, zrecv,
    e_sem, small_sem, bins_sem, z_ready, xc_ready, ysend_sem, yrecv_sem, fsend_sem, frecv_sem, legsend_sem, legrecv_sem,
    csend_sem, crecv_sem, xsend_sem, xrecv_sem, dsend_sem, drecv_sem, lsend_sem, lrecv_sem, zsend_sem, zrecv_sem,
):
    y = lax.axis_index("state")
    f = lax.axis_index("frame")
    core = lax.rem(f, 2)
    z = lax.rem(lax.div(f, 2), ZS)
    x = lax.div(f, 2 * ZS)
    width = COLS // PARTS
    x_at = [lax.rem(x + d, XS) * (2 * ZS) for d in range(XS)]
    z_at = [lax.rem(z + d, ZS) * 2 for d in range(ZS)]
    c_at = [core, 1 - core]
    y_near = [(lax.rem(y + d, YS), f) for d in (2, 1, 3)]
    z_near = [(y, x_at[0] + z_at[d] + core) for d in (2, 6, 1, 7)]
    xc_near = [
        (y, x_at[dx] + z_at[0] + c_at[dc]) for dx, dc in ((2, 1), (2, 0), (1, 1), (3, 1), (1, 0), (3, 0), (0, 1))
    ]

    barrier = pltpu.get_barrier_semaphore()
    for device in y_near + z_near + xc_near:
        pl.semaphore_signal(barrier, inc=1, device_id=device, device_id_type=MESH)

    n_load = pltpu.make_async_copy(n_hbm, n_ref, small_sem.at[0])
    n_load.start()
    loads = [
        pltpu.make_async_copy(
            e_hbm.at[:, pl.ds(i * width, width)], energies.at[:, pl.ds(i * width, width)], e_sem.at[i]
        )
        for i in range(PARTS)
    ]
    for load in loads:
        load.start()
    bins_load = pltpu.make_async_copy(bins_hbm, bins, bins_sem)
    bins_load.start()
    leg_load = pltpu.make_async_copy(leg_hbm, leg_ref, small_sem.at[1])
    leg_load.start()

    def count(first, last):
        def body(b, _):
            count_block(bins, counts, b)
            return 0

        lax.fori_loop(first, last, body, 0)

    def wide(col):
        return jnp.broadcast_to(col, (ROWS, LANES))

    def at(j):
        return pl.ds(pl.multiple_of(j * LANES, LANES), LANES)

    def eight(j):
        return pl.ds(pl.multiple_of(j * 8, 8), 8)

    def state_pass(first, last, scale=False):
        def body(k, _):
            for u in range(SPAN):
                j = k * SPAN + u
                pairs = []
                for h in range(2):
                    scores = []
                    for g in range(h * GROUPS // 2, (h + 1) * GROUPS // 2):
                        rows = pl.ds(8 * g, 8)
                        e = energies[rows, at(j)]
                        if scale:
                            e = e * -LOG2E
                            energies[rows, at(j)] = e
                        scores.append(terms[rows, :] + e)
                    pairs.append(online(scores))
                state_max[eight(j), :], state_sum[eight(j), :] = merged(pairs)
            return 0

        lax.fori_loop(first // SPAN, last // SPAN, body, 0)

    def y_send(stage, half):
        rows = [pl.ds(half * HALF * 8 + r, HALF, stride=8) for r in range(8)]
        largest, total = merged([(state_max[r, :], state_sum[r, :]) for r in rows])
        ybuf[stage, half, y] = largest + jnp.log(total) * LOG2E
        for device in y_near:
            pltpu.make_async_remote_copy(
                src_ref=ybuf.at[stage, half, y], dst_ref=ybuf.at[stage, half, y],
                send_sem=ysend_sem.at[stage, half], recv_sem=yrecv_sem.at[stage, half],
                device_id=device, device_id_type=MESH,
            ).start()

    def y_finish(stage, half):
        got = ybuf.at[stage, half, pl.ds(0, YS - 1)]
        pltpu.make_async_copy(got, got, yrecv_sem.at[stage, half]).wait()
        largest, total = online([ybuf[stage, half, k] for k in range(YS)])
        dbuf[pl.ds(half * HALF, HALF), :] = largest + jnp.log(total) * LOG2E

    def frame_pass(half):
        def body(b, _):
            divisors = [dbuf[pl.ds(b * SPAN + u, 1), :] for u in range(SPAN)]
            for g in range(GROUPS):
                rows = pl.ds(8 * g, 8)
                frame_max[b, rows, :], frame_sum[b, rows, :] = online(
                    [energies[rows, at(b * SPAN + u)] - divisors[u] for u in range(SPAN)]
                )
            return 0

        lax.fori_loop(half * HALF // SPAN, (half + 1) * HALF // SPAN, body, 0)

    frame_partners = sorted(
        [(dx, dz, dc) for dx in range(XS) for dz in range(ZS) for dc in range(2)],
        key=lambda k: min(k[0], XS - k[0]) + min(k[1], ZS - k[1]) + 0.5 * k[2],
        reverse=True,
    )[:-1]

    def f_send(stage):
        largest, total = merged([(frame_max[b], frame_sum[b]) for b in range(BLOCKS // SPAN)])
        most = jnp.max(largest, axis=1, keepdims=True)
        total = jnp.sum(total * jnp.exp2(largest - most), axis=1, keepdims=True)
        fbuf[stage, f] = to_row(most) + jnp.log(to_row(total)) * LOG2E
        for dx, dz, dc in frame_partners:
            pltpu.make_async_remote_copy(
                src_ref=fbuf.at[stage, f], dst_ref=fbuf.at[stage, f],
                send_sem=fsend_sem.at[stage], recv_sem=frecv_sem.at[stage],
                device_id=(y, x_at[dx] + z_at[dz] + c_at[dc]), device_id_type=MESH,
            ).start()

    def f_finish(stage):
        got = fbuf.at[stage, pl.ds(0, FS - 1)]
        pltpu.make_async_copy(got, got, frecv_sem.at[stage]).wait()
        parts = fbuf[stage]
        largest = jnp.max(parts, axis=0)
        return -(largest + jnp.log(jnp.sum(jnp.exp2(parts - largest[None]), axis=0)) * LOG2E)

    n_load.wait()
    log_counts = jnp.log(n_ref[...].astype(jnp.float32)) * LOG2E
    terms[...] = wide(to_col(log_counts))
    share = BLOCKS // PARTS
    loads[0].wait()
    state_pass(0, share, scale=True)
    loads[1].wait()
    state_pass(share, 2 * share, scale=True)
    pl.semaphore_wait(barrier, len(y_near + z_near + xc_near))
    for device in z_near[:2]:
        pl.semaphore_signal(z_ready, inc=1, device_id=device, device_id_type=MESH)
    y_send(0, 0)
    loads[2].wait()
    state_pass(2 * share, 3 * share, scale=True)
    loads[3].wait()
    state_pass(3 * share, 4 * share, scale=True)
    y_send(0, 1)
    bins_load.wait()
    count(0, 6)
    pl.semaphore_wait(z_ready, 2)
    for device in xc_near:
        pl.semaphore_signal(xc_ready, inc=1, device_id=device, device_id_type=MESH)
    y_finish(0, 0)
    frame_pass(0)
    y_finish(0, 1)
    frame_pass(1)
    pl.semaphore_wait(xc_ready, len(xc_near))
    f_send(0)
    count(6, 18)
    free = f_finish(0)

    terms[...] = wide(to_col(log_counts + free))
    state_pass(0, HALF)
    y_send(1, 0)
    state_pass(HALF, BLOCKS)
    y_send(1, 1)
    count(18, 24)
    y_finish(1, 0)
    frame_pass(0)
    y_finish(1, 1)
    frame_pass(1)
    f_send(1)
    count(24, COLS // WIDE)
    free = f_finish(1)

    terms[...] = wide(to_col(log_counts + free))
    state_pass(0, HALF)
    y_send(2, 0)
    state_pass(HALF, BLOCKS)
    y_send(2, 1)
    free_col = to_col(free)
    factors = wide(free_col)
    terms[...] = factors

    def weigh(j, _):
        value = jnp.exp2((terms[...] + energies[:, at(j)]) - dbuf[pl.ds(j, 1), :])
        weights[:, at(j)] = value.astype(jnp.bfloat16)
        return 0

    for half in range(2):
        y_finish(2, half)
        lax.fori_loop(half * HALF, (half + 1) * HALF, weigh, 0, unroll=SPAN)

    def offset(s):
        return 4 + (1 - 2 * lax.rem(s, 2)) * lax.div(s + 1, 2)

    def core_copy(s):
        other = 1 - core
        return pltpu.make_async_remote_copy(
            src_ref=part.at[s, :, other], dst_ref=crecv.at[s],
            send_sem=csend_sem, recv_sem=crecv_sem.at[s],
            device_id=(y, f + 1 - 2 * core), device_id_type=MESH,
        )

    def x_copy(s, d):
        to = lax.rem(x + d, XS)
        return pltpu.make_async_remote_copy(
            src_ref=xsend.at[s, to], dst_ref=xrecv.at[s, d - 1],
            send_sem=xsend_sem, recv_sem=xrecv_sem.at[s],
            device_id=(y, to * (2 * ZS) + z * 2 + core), device_id_type=MESH,
        )

    def near_copy(s, d):
        to = lax.rem(x + d, XS)
        to_z = lax.rem(z + offset(s), ZS)
        return pltpu.make_async_remote_copy(
            src_ref=xsend.at[s, to], dst_ref=drecv.at[s - FAR, d],
            send_sem=dsend_sem, recv_sem=drecv_sem.at[s - FAR],
            device_id=(y, to * (2 * ZS) + to_z * 2 + core), device_id_type=MESH,
        )

    def z_copy(s):
        to = lax.rem(z + offset(s), ZS)
        return pltpu.make_async_remote_copy(
            src_ref=zsend.at[s], dst_ref=zrecv.at[s],
            send_sem=zsend_sem, recv_sem=zrecv_sem,
            device_id=(y, x * (2 * ZS) + to * 2 + core), device_id_type=MESH,
        )

    def core_post(s):
        pltpu.make_async_copy(crecv.at[s], crecv.at[s], crecv_sem.at[s]).wait()
        xsend[s] = part[s, :, core] + crecv[s]

    def far_post(s):
        core_post(s)
        for d in (2, 1, 3):
            x_copy(s, d).start()

    def near_post(s):
        core_post(s)
        for d in (2, 1, 3, 0):
            near_copy(s, d).start()

    def x_post(s):
        pltpu.make_async_copy(xrecv.at[s], xrecv.at[s], xrecv_sem.at[s]).wait()
        zsend[s] = (xsend[s, x] + xrecv[s, 0]) + (xrecv[s, 1] + xrecv[s, 2])
        z_copy(s).start()

    lag = 5

    last = ZS - 1

    def product(s, frames):
        rows = pl.ds(pl.multiple_of(lax.rem(z + offset(s), ZS) * (XS * 2 * OWN), 32), XS * 2 * OWN)
        result = lax.dot_general(
            counts[rows, frames], weights[:, frames], (((1,), (1,)), ((), ())), preferred_element_type=jnp.float32
        )
        return result.reshape(XS, 2, OWN, LANES)

    def step(s, _):
        part[s] = product(s, slice(None))
        core_copy(s).start()

        @pl.when(jnp.logical_and(s >= 1, s <= FAR))
        def _():
            far_post(s - 1)

        @pl.when(s > FAR)
        def _():
            near_post(s - 1)

        @pl.when(s >= lag)
        def _():
            x_post(s - lag)

        return 0

    lax.fori_loop(0, last, step, 0)
    part[last] = product(last, slice(None))
    near_post(last - 1)
    last_partners = [(2, 1), (2, 0), (1, 1), (3, 1), (1, 0), (3, 0), (0, 1)]
    for k, (dx, dc) in enumerate(last_partners):
        c = c_at[dc]
        pltpu.make_async_remote_copy(
            src_ref=part.at[last, lax.rem(x + dx, XS), c], dst_ref=lrecv.at[k],
            send_sem=lsend_sem, recv_sem=lrecv_sem,
            device_id=(y, x_at[dx] + z_at[0] + c), device_id_type=MESH,
        ).start()

    leg_load.wait()
    leg_col = to_col(leg_ref[...].astype(jnp.float32))
    lane = lax.broadcasted_iota(jnp.int32, (ROWS, LANES), 1).astype(jnp.float32)
    table = (wide(leg_col) == lane).astype(jnp.float32)
    legbuf[y, 0:1] = jnp.sum(table * factors, axis=0, keepdims=True)
    legbuf[y, 1:2] = jnp.sum(table, axis=0, keepdims=True)
    for device in y_near:
        pltpu.make_async_remote_copy(
            src_ref=legbuf.at[y], dst_ref=legbuf.at[y],
            send_sem=legsend_sem, recv_sem=legrecv_sem,
            device_id=device, device_id_type=MESH,
        ).start()
    got = zrecv.at[pl.ds(0, FAR)]
    pltpu.make_async_copy(got, got, zrecv_sem).wait()
    total = part[last, x, core]
    for s in range(FAR):
        total = total + zrecv[s]
    for s in range(FAR, last):
        got = drecv.at[s - FAR]
        pltpu.make_async_copy(got, got, drecv_sem.at[s - FAR]).wait()
        for d in range(XS):
            total = total + drecv[s - FAR, d]
    pltpu.make_async_copy(lrecv, lrecv, lrecv_sem).wait()
    for k in range(len(last_partners)):
        total = total + lrecv[k]
    out_ref[0:OWN, :] = total * (BINS / PAIRS)
    got = legbuf.at[pl.ds(0, YS - 1)]
    pltpu.make_async_copy(got, got, legrecv_sem).wait()
    legs = (legbuf[0] + legbuf[1]) + (legbuf[2] + legbuf[3])
    leg_mean = legs[0:1] / jnp.maximum(legs[1:2], 1.0)
    own_mean = jnp.sum(table * jnp.broadcast_to(leg_mean, (ROWS, LANES)), axis=1, keepdims=True)
    out_ref[OWN : OWN + 8, :] = jnp.broadcast_to(to_row((free_col - own_mean) * LN2), (8, LANES))

    for stage in range(ITERS + 1):
        for half in range(2):
            sent = ybuf.at[stage, half, pl.ds(0, YS - 1)]
            pltpu.make_async_copy(sent, sent, ysend_sem.at[stage, half]).wait()
    for stage in range(ITERS):
        sent = fbuf.at[stage, pl.ds(0, FS - 1)]
        pltpu.make_async_copy(sent, sent, fsend_sem.at[stage]).wait()
    sent = legbuf.at[pl.ds(0, YS - 1)]
    pltpu.make_async_copy(sent, sent, legsend_sem).wait()
    pltpu.make_async_copy(crecv, crecv, csend_sem).wait()
    pltpu.make_async_copy(xrecv, xrecv, xsend_sem).wait()
    pltpu.make_async_copy(drecv, drecv, dsend_sem).wait()
    pltpu.make_async_copy(lrecv, lrecv, lsend_sem).wait()
    sent = zrecv.at[pl.ds(0, FAR)]
    pltpu.make_async_copy(sent, sent, zsend_sem).wait()


def split(both_ref, rdf_ref, leg_ref):
    rdf_ref[...] = both_ref[0:OWN, :]
    leg_ref[...] = both_ref[OWN : OWN + 1, :]


def local(energies, sample_counts, state_leg, bin_index):
    hbm = pl.BlockSpec(memory_space=pl.ANY)
    vmem = pl.BlockSpec(memory_space=pltpu.VMEM)
    f32 = jnp.float32
    dma = pltpu.SemaphoreType.DMA
    both = pl.pallas_call(
        kernel,
        out_shape=jax.ShapeDtypeStruct((OWN + 8, LANES), f32),
        in_specs=[hbm] * 4,
        out_specs=vmem,
        scratch_shapes=[
            pltpu.VMEM((ROWS, COLS), f32),
            pltpu.VMEM((1, LANES), jnp.int32),
            pltpu.VMEM((1, LANES), jnp.int32),
            pltpu.VMEM((TYPES, PAIRS, COLS), jnp.int32),
            pltpu.VMEM((TYPES * BINS, COLS), jnp.bfloat16),
            pltpu.VMEM((ROWS, COLS), jnp.bfloat16),
            pltpu.VMEM((ROWS, LANES), f32),
            pltpu.VMEM((BLOCKS * 8, LANES), f32),
            pltpu.VMEM((BLOCKS * 8, LANES), f32),
            pltpu.VMEM((BLOCKS // SPAN, ROWS, LANES), f32),
            pltpu.VMEM((BLOCKS // SPAN, ROWS, LANES), f32),
            pltpu.VMEM((BLOCKS, LANES), f32),
            pltpu.VMEM((ITERS + 1, 2, YS, HALF, LANES), f32),
            pltpu.VMEM((ITERS, FS, 1, LANES), f32),
            pltpu.VMEM((YS, 2, LANES), f32),
            pltpu.VMEM((ZS, XS, 2, OWN, LANES), f32),
            pltpu.VMEM((ZS - 1, XS, OWN, LANES), f32),
            pltpu.VMEM((ZS - 1, XS, OWN, LANES), f32),
            pltpu.VMEM((FAR, XS - 1, OWN, LANES), f32),
            pltpu.VMEM((ZS - 1 - FAR, XS, OWN, LANES), f32),
            pltpu.VMEM((2 * XS - 1, OWN, LANES), f32),
            pltpu.VMEM((FAR, OWN, LANES), f32),
            pltpu.VMEM((FAR, OWN, LANES), f32),
            dma((PARTS,)),
            dma((2,)),
            dma,
            pltpu.SemaphoreType.REGULAR,
            pltpu.SemaphoreType.REGULAR,
            dma((ITERS + 1, 2)),
            dma((ITERS + 1, 2)),
            dma((ITERS,)),
            dma((ITERS,)),
            dma,
            dma,
            dma,
            dma((ZS - 1,)),
            dma,
            dma((FAR,)),
            dma,
            dma((ZS - 1 - FAR,)),
            dma,
            dma,
            dma,
            dma,
        ],
        compiler_params=pltpu.CompilerParams(
            collective_id=0, has_side_effects=True, vmem_limit_bytes=56 * 2**20
        ),
        name="reweight",
    )(
        energies,
        sample_counts.reshape(1, LANES),
        state_leg.reshape(1, LANES),
        jnp.transpose(bin_index, (1, 2, 0)),
    )
    rdf, leg_free = pl.pallas_call(
        split,
        out_shape=(jax.ShapeDtypeStruct((OWN, LANES), f32), jax.ShapeDtypeStruct((1, LANES), f32)),
        in_specs=[vmem],
        out_specs=(vmem, vmem),
        name="split",
    )(both)
    return rdf, leg_free.reshape(LANES)


def solution(mesh):
    placed = (P("state", "frame"), P("state"), P("state"), P("frame", None, None))
    return jax.shard_map(
        local,
        mesh=mesh,
        in_specs=placed,
        out_specs=(P("frame", "state"), P("state")),
        check_vma=False,
    )
```

```python
import functools

import jax
import jax.numpy as jnp
from jax import lax
from jax.experimental import pallas as pl
from jax.experimental.pallas import tpu as pltpu
from jax.sharding import PartitionSpec as P

BINS = 256
TYPES = 6
PAIRS = 8
LEGS = 8
ITERS = 2
YS = 4
XS = 4
ZS = 8
FS = XS * ZS * 2
LANES = 128
ROWS = 128
COLS = 8192
BLOCKS = COLS // LANES
OWN = TYPES * BINS // FS
PARTS = 4
GROUPS = ROWS // 8
WIDE = 256
LOG2E = 1.4426950408889634
LN2 = 0.6931471805599453
UNROLL = 4
HALF = BLOCKS // 2
SPAN = 8
FAR = 2
MESH = pl.DeviceIdType.MESH


def eye():
    shape = (ROWS, LANES)
    return lax.broadcasted_iota(jnp.int32, shape, 0) == lax.broadcasted_iota(jnp.int32, shape, 1)


def to_col(row):
    return jnp.sum(jnp.where(eye(), jnp.broadcast_to(row, (ROWS, LANES)), 0.0), axis=1, keepdims=True)


def to_row(col):
    return jnp.sum(jnp.where(eye(), jnp.broadcast_to(col, (ROWS, LANES)), 0.0), axis=0, keepdims=True)


def place(row):
    group, rest = divmod(row, 2 * OWN)
    x, z = divmod(group, ZS)
    return z * (XS * 2 * OWN) + x * 2 * OWN + rest


def count_block(bins, counts, block):
    cols = pl.ds(pl.multiple_of(block * WIDE, WIDE), WIDE)
    iota = lax.broadcasted_iota(jnp.int32, (16, WIDE), 0)
    for t in range(TYPES):
        rows = bins[t, :, cols]
        low = rows & 15
        one = jnp.left_shift(1, (rows >> 4) * 2)
        even = odd = None
        for group in ((0, 1, 2), (3, 4, 5), (6, 7)):
            word = None
            for p in group:
                hot = jnp.where(low[p : p + 1] == iota, one[p : p + 1], 0)
                word = hot if word is None else word + hot
            a = word & 0x33333333
            b = lax.shift_right_logical(word, 2) & 0x33333333
            even = a if even is None else even + a
            odd = b if odd is None else odd + b
        for half, nibbles in ((0, even), (16, odd)):
            for q in range(0, 8, 2):
                v = lax.shift_right_logical(nibbles, 4 * q) if q else nibbles
                if q < 6:
                    v = v & 255
                v = v.astype(jnp.float32).astype(jnp.bfloat16)
                upper = (v + jnp.bfloat16(2048)) - jnp.bfloat16(2048)
                base = t * BINS + 32 * q + half
                counts[pl.ds(place(base), 16), cols] = v - upper
                counts[pl.ds(place(base + 32), 16), cols] = upper * jnp.bfloat16(0.0625)


def online(parts):
    largest = functools.reduce(jnp.maximum, parts)
    return largest, functools.reduce(jnp.add, [jnp.exp2(part - largest) for part in parts])


def merged(pairs):
    largest = functools.reduce(jnp.maximum, [m for m, _ in pairs])
    return largest, functools.reduce(jnp.add, [s * jnp.exp2(m - largest) for m, s in pairs])


def kernel(
    e_hbm, n_hbm, leg_hbm, bins_hbm, out_ref,
    energies, n_ref, leg_ref, bins, counts, weights, terms, state_max, state_sum, frame_max, frame_sum, dbuf,
    ybuf, fbuf, legbuf, part, crecv, xsend, xrecv, drecv, lrecv, zsend, zrecv,
    e_sem, small_sem, bins_sem, z_ready, xc_ready, ysend_sem, yrecv_sem, fsend_sem, frecv_sem, legsend_sem, legrecv_sem,
    csend_sem, crecv_sem, xsend_sem, xrecv_sem, dsend_sem, drecv_sem, lsend_sem, lrecv_sem, zsend_sem, zrecv_sem,
):
    y = lax.axis_index("state")
    f = lax.axis_index("frame")
    core = lax.rem(f, 2)
    z = lax.rem(lax.div(f, 2), ZS)
    x = lax.div(f, 2 * ZS)
    width = COLS // PARTS
    x_at = [lax.rem(x + d, XS) * (2 * ZS) for d in range(XS)]
    z_at = [lax.rem(z + d, ZS) * 2 for d in range(ZS)]
    c_at = [core, 1 - core]
    y_near = [(lax.rem(y + d, YS), f) for d in (2, 1, 3)]
    z_near = [(y, x_at[0] + z_at[d] + core) for d in (2, 6, 1, 7)]
    xc_near = [
        (y, x_at[dx] + z_at[0] + c_at[dc]) for dx, dc in ((2, 1), (2, 0), (1, 1), (3, 1), (1, 0), (3, 0), (0, 1))
    ]

    barrier = pltpu.get_barrier_semaphore()
    for device in y_near + z_near + xc_near:
        pl.semaphore_signal(barrier, inc=1, device_id=device, device_id_type=MESH)

    n_load = pltpu.make_async_copy(n_hbm, n_ref, small_sem.at[0])
    n_load.start()
    loads = [
        pltpu.make_async_copy(
            e_hbm.at[:, pl.ds(i * width, width)], energies.at[:, pl.ds(i * width, width)], e_sem.at[i]
        )
        for i in range(PARTS)
    ]
    for load in loads:
        load.start()
    bins_load = pltpu.make_async_copy(bins_hbm, bins, bins_sem)
    bins_load.start()
    leg_load = pltpu.make_async_copy(leg_hbm, leg_ref, small_sem.at[1])
    leg_load.start()

    def count(first, last):
        def body(b, _):
            count_block(bins, counts, b)
            return 0

        lax.fori_loop(first, last, body, 0)

    def wide(col):
        return jnp.broadcast_to(col, (ROWS, LANES))

    def at(j):
        return pl.ds(pl.multiple_of(j * LANES, LANES), LANES)

    def eight(j):
        return pl.ds(pl.multiple_of(j * 8, 8), 8)

    def state_pass(first, last, scale=False):
        def body(k, _):
            for u in range(SPAN):
                j = k * SPAN + u
                pairs = []
                for h in range(2):
                    scores = []
                    for g in range(h * GROUPS // 2, (h + 1) * GROUPS // 2):
                        rows = pl.ds(8 * g, 8)
                        e = energies[rows, at(j)]
                        if scale:
                            e = e * -LOG2E
                            energies[rows, at(j)] = e
                        scores.append(terms[rows, :] + e)
                    pairs.append(online(scores))
                state_max[eight(j), :], state_sum[eight(j), :] = merged(pairs)
            return 0

        lax.fori_loop(first // SPAN, last // SPAN, body, 0)

    def y_send(stage, half):
        rows = [pl.ds(half * HALF * 8 + r, HALF, stride=8) for r in range(8)]
        largest, total = merged([(state_max[r, :], state_sum[r, :]) for r in rows])
        ybuf[stage, half, y] = largest + jnp.log(total) * LOG2E
        for device in y_near:
            pltpu.make_async_remote_copy(
                src_ref=ybuf.at[stage, half, y], dst_ref=ybuf.at[stage, half, y],
                send_sem=ysend_sem.at[stage, half], recv_sem=yrecv_sem.at[stage, half],
                device_id=device, device_id_type=MESH,
            ).start()

    def y_finish(stage, half):
        got = ybuf.at[stage, half, pl.ds(0, YS - 1)]
        pltpu.make_async_copy(got, got, yrecv_sem.at[stage, half]).wait()
        largest, total = online([ybuf[stage, half, k] for k in range(YS)])
        dbuf[pl.ds(half * HALF, HALF), :] = largest + jnp.log(total) * LOG2E

    def frame_pass(half):
        def body(b, _):
            divisors = [dbuf[pl.ds(b * SPAN + u, 1), :] for u in range(SPAN)]
            for g in range(GROUPS):
                rows = pl.ds(8 * g, 8)
                frame_max[b, rows, :], frame_sum[b, rows, :] = online(
                    [energies[rows, at(b * SPAN + u)] - divisors[u] for u in range(SPAN)]
                )
            return 0

        lax.fori_loop(half * HALF // SPAN, (half + 1) * HALF // SPAN, body, 0)

    frame_partners = sorted(
        [(dx, dz, dc) for dx in range(XS) for dz in range(ZS) for dc in range(2)],
        key=lambda k: min(k[0], XS - k[0]) + min(k[1], ZS - k[1]) + 0.5 * k[2],
        reverse=True,
    )[:-1]

    def f_send(stage):
        largest, total = merged([(frame_max[b], frame_sum[b]) for b in range(BLOCKS // SPAN)])
        most = jnp.max(largest, axis=1, keepdims=True)
        total = jnp.sum(total * jnp.exp2(largest - most), axis=1, keepdims=True)
        fbuf[stage, f] = to_row(most) + jnp.log(to_row(total)) * LOG2E
        for dx, dz, dc in frame_partners:
            pltpu.make_async_remote_copy(
                src_ref=fbuf.at[stage, f], dst_ref=fbuf.at[stage, f],
                send_sem=fsend_sem.at[stage], recv_sem=frecv_sem.at[stage],
                device_id=(y, x_at[dx] + z_at[dz] + c_at[dc]), device_id_type=MESH,
            ).start()

    def f_finish(stage):
        got = fbuf.at[stage, pl.ds(0, FS - 1)]
        pltpu.make_async_copy(got, got, frecv_sem.at[stage]).wait()
        parts = fbuf[stage]
        largest = jnp.max(parts, axis=0)
        return -(largest + jnp.log(jnp.sum(jnp.exp2(parts - largest[None]), axis=0)) * LOG2E)

    n_load.wait()
    log_counts = jnp.log(n_ref[...].astype(jnp.float32)) * LOG2E
    terms[...] = wide(to_col(log_counts))
    share = BLOCKS // PARTS
    loads[0].wait()
    state_pass(0, share, scale=True)
    loads[1].wait()
    state_pass(share, 2 * share, scale=True)
    pl.semaphore_wait(barrier, len(y_near + z_near + xc_near))
    for device in z_near[:2]:
        pl.semaphore_signal(z_ready, inc=1, device_id=device, device_id_type=MESH)
    y_send(0, 0)
    loads[2].wait()
    state_pass(2 * share, 3 * share, scale=True)
    loads[3].wait()
    state_pass(3 * share, 4 * share, scale=True)
    y_send(0, 1)
    bins_load.wait()
    count(0, 6)
    pl.semaphore_wait(z_ready, 2)
    for device in xc_near:
        pl.semaphore_signal(xc_ready, inc=1, device_id=device, device_id_type=MESH)
    y_finish(0, 0)
    frame_pass(0)
    y_finish(0, 1)
    frame_pass(1)
    pl.semaphore_wait(xc_ready, len(xc_near))
    f_send(0)
    count(6, 18)
    free = f_finish(0)

    terms[...] = wide(to_col(log_counts + free))
    state_pass(0, HALF)
    y_send(1, 0)
    state_pass(HALF, BLOCKS)
    y_send(1, 1)
    count(18, 24)
    y_finish(1, 0)
    frame_pass(0)
    y_finish(1, 1)
    frame_pass(1)
    f_send(1)
    count(24, COLS // WIDE)
    free = f_finish(1)

    terms[...] = wide(to_col(log_counts + free))
    state_pass(0, HALF)
    y_send(2, 0)
    state_pass(HALF, BLOCKS)
    y_send(2, 1)
    free_col = to_col(free)
    factors = wide(free_col)
    terms[...] = factors

    def weigh(j, _):
        value = jnp.exp2((terms[...] + energies[:, at(j)]) - dbuf[pl.ds(j, 1), :])
        weights[:, at(j)] = value.astype(jnp.bfloat16)
        return 0

    for half in range(2):
        y_finish(2, half)
        lax.fori_loop(half * HALF, (half + 1) * HALF, weigh, 0, unroll=SPAN)

    def offset(s):
        return 4 + (1 - 2 * lax.rem(s, 2)) * lax.div(s + 1, 2)

    def core_copy(s):
        other = 1 - core
        return pltpu.make_async_remote_copy(
            src_ref=part.at[s, :, other], dst_ref=crecv.at[s],
            send_sem=csend_sem, recv_sem=crecv_sem.at[s],
            device_id=(y, f + 1 - 2 * core), device_id_type=MESH,
        )

    def x_copy(s, d):
        to = lax.rem(x + d, XS)
        return pltpu.make_async_remote_copy(
            src_ref=xsend.at[s, to], dst_ref=xrecv.at[s, d - 1],
            send_sem=xsend_sem, recv_sem=xrecv_sem.at[s],
            device_id=(y, to * (2 * ZS) + z * 2 + core), device_id_type=MESH,
        )

    def near_copy(s, d):
        to = lax.rem(x + d, XS)
        to_z = lax.rem(z + offset(s), ZS)
        return pltpu.make_async_remote_copy(
            src_ref=xsend.at[s, to], dst_ref=drecv.at[s - FAR, d],
            send_sem=dsend_sem, recv_sem=drecv_sem.at[s - FAR],
            device_id=(y, to * (2 * ZS) + to_z * 2 + core), device_id_type=MESH,
        )

    def z_copy(s):
        to = lax.rem(z + offset(s), ZS)
        return pltpu.make_async_remote_copy(
            src_ref=zsend.at[s], dst_ref=zrecv.at[s],
            send_sem=zsend_sem, recv_sem=zrecv_sem,
            device_id=(y, x * (2 * ZS) + to * 2 + core), device_id_type=MESH,
        )

    def core_post(s):
        pltpu.make_async_copy(crecv.at[s], crecv.at[s], crecv_sem.at[s]).wait()

    def far_post(s):
        core_post(s)
        xsend[s, x] = part[s, x, core] + crecv[s, x]
        for d in (2, 1, 3):
            to = lax.rem(x + d, XS)
            xsend[s, to] = part[s, to, core] + crecv[s, to]
            x_copy(s, d).start()

    def near_post(s):
        core_post(s)
        for d in (2, 1, 3, 0):
            to = lax.rem(x + d, XS)
            xsend[s, to] = part[s, to, core] + crecv[s, to]
            near_copy(s, d).start()

    def x_post(s):
        pltpu.make_async_copy(xrecv.at[s], xrecv.at[s], xrecv_sem.at[s]).wait()
        zsend[s] = (xsend[s, x] + xrecv[s, 0]) + (xrecv[s, 1] + xrecv[s, 2])
        z_copy(s).start()

    lag = 4

    last = ZS - 1

    def product(s, frames):
        rows = pl.ds(pl.multiple_of(lax.rem(z + offset(s), ZS) * (XS * 2 * OWN), 32), XS * 2 * OWN)
        result = lax.dot_general(
            counts[rows, frames], weights[:, frames], (((1,), (1,)), ((), ())), preferred_element_type=jnp.float32
        )
        return result.reshape(XS, 2, OWN, LANES)

    def step(s, _):
        part[s] = product(s, slice(None))
        core_copy(s).start()

        @pl.when(jnp.logical_and(s >= 1, s <= FAR))
        def _():
            far_post(s - 1)

        @pl.when(s > FAR)
        def _():
            near_post(s - 1)

        @pl.when(jnp.logical_and(s >= lag, s < lag + FAR))
        def _():
            x_post(s - lag)

        return 0

    lax.fori_loop(0, last, step, 0)
    part[last] = product(last, slice(None))
    near_post(last - 1)
    last_partners = [(2, 1), (2, 0), (1, 1), (3, 1), (1, 0), (3, 0), (0, 1)]
    for k, (dx, dc) in enumerate(last_partners):
        c = c_at[dc]
        pltpu.make_async_remote_copy(
            src_ref=part.at[last, lax.rem(x + dx, XS), c], dst_ref=lrecv.at[k],
            send_sem=lsend_sem, recv_sem=lrecv_sem,
            device_id=(y, x_at[dx] + z_at[0] + c), device_id_type=MESH,
        ).start()

    leg_load.wait()
    leg_col = to_col(leg_ref[...].astype(jnp.float32))
    lane = lax.broadcasted_iota(jnp.int32, (ROWS, LANES), 1).astype(jnp.float32)
    table = (wide(leg_col) == lane).astype(jnp.float32)
    legbuf[y, 0:1] = jnp.sum(table * factors, axis=0, keepdims=True)
    legbuf[y, 1:2] = jnp.sum(table, axis=0, keepdims=True)
    for device in y_near:
        pltpu.make_async_remote_copy(
            src_ref=legbuf.at[y], dst_ref=legbuf.at[y],
            send_sem=legsend_sem, recv_sem=legrecv_sem,
            device_id=device, device_id_type=MESH,
        ).start()
    got = zrecv.at[pl.ds(0, FAR)]
    pltpu.make_async_copy(got, got, zrecv_sem).wait()
    total = part[last, x, core]
    for s in range(FAR):
        total = total + zrecv[s]
    for s in range(FAR, last):
        got = drecv.at[s - FAR]
        pltpu.make_async_copy(got, got, drecv_sem.at[s - FAR]).wait()
        for d in range(XS):
            total = total + drecv[s - FAR, d]
    pltpu.make_async_copy(lrecv, lrecv, lrecv_sem).wait()
    for k in range(len(last_partners)):
        total = total + lrecv[k]
    out_ref[0:OWN, :] = total * (BINS / PAIRS)
    got = legbuf.at[pl.ds(0, YS - 1)]
    pltpu.make_async_copy(got, got, legrecv_sem).wait()
    legs = (legbuf[0] + legbuf[1]) + (legbuf[2] + legbuf[3])
    leg_mean = legs[0:1] / jnp.maximum(legs[1:2], 1.0)
    own_mean = jnp.sum(table * jnp.broadcast_to(leg_mean, (ROWS, LANES)), axis=1, keepdims=True)
    out_ref[OWN : OWN + 8, :] = jnp.broadcast_to(to_row((free_col - own_mean) * LN2), (8, LANES))

    for stage in range(ITERS + 1):
        for half in range(2):
            sent = ybuf.at[stage, half, pl.ds(0, YS - 1)]
            pltpu.make_async_copy(sent, sent, ysend_sem.at[stage, half]).wait()
    for stage in range(ITERS):
        sent = fbuf.at[stage, pl.ds(0, FS - 1)]
        pltpu.make_async_copy(sent, sent, fsend_sem.at[stage]).wait()
    sent = legbuf.at[pl.ds(0, YS - 1)]
    pltpu.make_async_copy(sent, sent, legsend_sem).wait()
    pltpu.make_async_copy(crecv, crecv, csend_sem).wait()
    pltpu.make_async_copy(xrecv, xrecv, xsend_sem).wait()
    pltpu.make_async_copy(drecv, drecv, dsend_sem).wait()
    pltpu.make_async_copy(lrecv, lrecv, lsend_sem).wait()
    sent = zrecv.at[pl.ds(0, FAR)]
    pltpu.make_async_copy(sent, sent, zsend_sem).wait()


def split(both_ref, rdf_hbm, leg_hbm, sem):
    copies = [
        pltpu.make_async_copy(both_ref.at[pl.ds(0, OWN)], rdf_hbm, sem.at[0]),
        pltpu.make_async_copy(both_ref.at[pl.ds(OWN, 1)], leg_hbm, sem.at[1]),
    ]
    for copy in copies:
        copy.start()
    for copy in copies:
        copy.wait()


def local(energies, sample_counts, state_leg, bin_index):
    hbm = pl.BlockSpec(memory_space=pl.ANY)
    vmem = pl.BlockSpec(memory_space=pltpu.VMEM)
    f32 = jnp.float32
    dma = pltpu.SemaphoreType.DMA
    both = pl.pallas_call(
        kernel,
        out_shape=pltpu.VMEM((OWN + 8, LANES), f32),
        in_specs=[hbm] * 4,
        out_specs=vmem,
        scratch_shapes=[
            pltpu.VMEM((ROWS, COLS), f32),
            pltpu.VMEM((1, LANES), jnp.int32),
            pltpu.VMEM((1, LANES), jnp.int32),
            pltpu.VMEM((TYPES, PAIRS, COLS), jnp.int32),
            pltpu.VMEM((TYPES * BINS, COLS), jnp.bfloat16),
            pltpu.VMEM((ROWS, COLS), jnp.bfloat16),
            pltpu.VMEM((ROWS, LANES), f32),
            pltpu.VMEM((BLOCKS * 8, LANES), f32),
            pltpu.VMEM((BLOCKS * 8, LANES), f32),
            pltpu.VMEM((BLOCKS // SPAN, ROWS, LANES), f32),
            pltpu.VMEM((BLOCKS // SPAN, ROWS, LANES), f32),
            pltpu.VMEM((BLOCKS, LANES), f32),
            pltpu.VMEM((ITERS + 1, 2, YS, HALF, LANES), f32),
            pltpu.VMEM((ITERS, FS, 1, LANES), f32),
            pltpu.VMEM((YS, 2, LANES), f32),
            pltpu.VMEM((ZS, XS, 2, OWN, LANES), f32),
            pltpu.VMEM((ZS - 1, XS, OWN, LANES), f32),
            pltpu.VMEM((ZS - 1, XS, OWN, LANES), f32),
            pltpu.VMEM((FAR, XS - 1, OWN, LANES), f32),
            pltpu.VMEM((ZS - 1 - FAR, XS, OWN, LANES), f32),
            pltpu.VMEM((2 * XS - 1, OWN, LANES), f32),
            pltpu.VMEM((FAR, OWN, LANES), f32),
            pltpu.VMEM((FAR, OWN, LANES), f32),
            dma((PARTS,)),
            dma((2,)),
            dma,
            pltpu.SemaphoreType.REGULAR,
            pltpu.SemaphoreType.REGULAR,
            dma((ITERS + 1, 2)),
            dma((ITERS + 1, 2)),
            dma((ITERS,)),
            dma((ITERS,)),
            dma,
            dma,
            dma,
            dma((ZS - 1,)),
            dma,
            dma((FAR,)),
            dma,
            dma((ZS - 1 - FAR,)),
            dma,
            dma,
            dma,
            dma,
        ],
        compiler_params=pltpu.CompilerParams(
            collective_id=0, has_side_effects=True, vmem_limit_bytes=56 * 2**20
        ),
        name="reweight",
    )(
        energies,
        sample_counts.reshape(1, LANES),
        state_leg.reshape(1, LANES),
        jnp.transpose(bin_index, (1, 2, 0)),
    )
    rdf, leg_free = pl.pallas_call(
        split,
        out_shape=(jax.ShapeDtypeStruct((OWN, LANES), f32), jax.ShapeDtypeStruct((1, LANES), f32)),
        in_specs=[vmem],
        out_specs=(hbm, hbm),
        scratch_shapes=[dma((2,))],
        name="split",
    )(both)
    return rdf, leg_free.reshape(LANES)


def solution(mesh):
    placed = (P("state", "frame"), P("state"), P("state"), P("frame", None, None))
    return jax.shard_map(
        local,
        mesh=mesh,
        in_specs=placed,
        out_specs=(P("frame", "state"), P("state")),
        check_vma=False,
    )
```
